32 devices in a mesh: gx: 4 (over y, x), gy: 8 (over z, core).
Axes of the slice: x: 2, y: 2, z: 4, core: 2. Of those that a mesh axis runs over, the one named last changes fastest.
Arguments:
- source: float32 [2, 256, 64, 512], P(None, ('gx', 'gy')), may hold values from -6 to 6
- weights: float32 [5, 2, 256, 64, 128], P(None, None, ('gx', 'gy')), may hold values from -0.375 to 0.375
- interp: float32 [2, 256, 64, 128], P(None, ('gx', 'gy')), may hold values from -0.5 to 0.5
Outputs:
- far_field: float32 [2, 512, 256, 128], P(None, ('gx', 'gy'))
The draws below stay inside these ranges and needn't reach their ends.
All inputs are finite; a program needn't handle non-finite values.
Results may differ from the reference program's by a relative error of at most 0.0001.
Values sent between devices are 32-bit elements; how exact they have to be, the bound alone decides.
A program may use at most 64 MiB of HBM per device.

```python
import jax
import jax.numpy as jnp
from jax import lax

R = 64
Q = 128
K = 8
S = 512
P_SIZE = 256
LV = 5


def block_scale(stream_key, extent, cuts, least, top_value):
    def one(axis_at, shards_of):
        steps = jax.random.uniform(jax.random.fold_in(jax.random.fold_in(stream_key, 6), axis_at), (shards_of,), jnp.float32, least / len(cuts), top_value / len(cuts))
        return jnp.repeat(jnp.exp(steps), extent[axis_at] // shards_of).reshape((-1,) + (1,) * (len(extent) - axis_at - 1))

    factor_of = one(*cuts[0])
    for cut in cuts[1:]:
        factor_of = factor_of * one(*cut)
    return factor_of


def scatter_about(key, shape, scale, bound, cuts=(), held_as=jnp.bfloat16):
    loudness = block_scale(key, shape, cuts, -0.22, 0.18) if cuts else 1.0
    array = jax.random.normal(key, shape, jnp.float32) * scale * loudness
    return jnp.minimum(jnp.maximum(array, -bound), bound).astype(held_as)


def setup_inputs(seed: int = 0) -> dict:
    key_of = jax.random.split(jax.random.key(seed), 4)
    return {
        "source": scatter_about(key_of[0], (2, P_SIZE, R, S), 1.0, 6.0, ((1, 32),), jnp.float32),
        "weights": scatter_about(key_of[1], (LV, 2, P_SIZE, R, 2 * R), (4 * R) ** -0.5, 0.375, ((2, 32),), jnp.float32),
        "interp": scatter_about(key_of[2], (2, P_SIZE, R, Q), (2 * R) ** -0.5, 0.5, ((1, 32),), jnp.float32),
    }


def mix(w_part, c_part):
    return jnp.einsum('gbmrj,gmjs->gbmrs', w_part, c_part, precision=lax.Precision.HIGHEST)


def reference(source, weights, interp):
    state = source
    for level in range(LV):
        span = K * 2 ** level
        groups = P_SIZE // (2 * span)
        split = state.reshape(2, groups, 2, span, R, S)
        stacked = jnp.concatenate([split[:, :, 0], split[:, :, 1]], axis=3)
        blocks = weights[level].reshape(2, groups, 2, span, R, 2 * R)
        real = mix(blocks[0], stacked[0]) - mix(blocks[1], stacked[1])
        imag = mix(blocks[0], stacked[1]) + mix(blocks[1], stacked[0])
        state = jnp.stack([real, imag]).reshape(2, P_SIZE, R, S)

    def proj(a, b):
        return jnp.einsum('prq,prs->spq', a, b, precision=lax.Precision.HIGHEST)

    real = proj(interp[0], state[0]) - proj(interp[1], state[1])
    imag = proj(interp[0], state[1]) + proj(interp[1], state[0])
    return jnp.stack([real, imag])
```

```python
import functools

import jax
import jax.numpy as jnp
from jax import lax
from jax.experimental import pallas as pl
from jax.experimental.pallas import tpu as pltpu
from jax.sharding import PartitionSpec as P

MESH = pl.DeviceIdType.MESH
BF = jnp.bfloat16
F32 = jnp.float32


def split(x):
    hi = x.astype(BF)
    return hi, (x - hi.astype(F32)).astype(BF)


def mul3(x, both, width):
    hi, lo = split(x)
    wide = jnp.dot(hi, both, preferred_element_type=F32)
    return wide[:, :width] + (
        wide[:, width:] + jnp.dot(lo, both[:, :width], preferred_element_type=F32)
    )


def kernel(ngx, ngy, halves, source, weights, interp, out, wp, ip, held, got, stage,
           send_sem, recv_sem, put_sem, take_sem, own_sem):
    n = ngx * ngy
    levels = weights.shape[0]
    boxes, rank, frames = source.shape[1:]
    q = interp.shape[3]
    per = frames // n // halves
    rows = frames // halves
    chunks = halves * boxes
    bits_gy = ngy.bit_length() - 1
    gx, gy = lax.axis_index("gx"), lax.axis_index("gy")
    me = gx * ngy + gy

    barrier = pltpu.get_barrier_semaphore()

    def greet(i, _):
        there = lax.rem(me + i, n)
        pl.semaphore_signal(barrier, inc=1, device_id=(lax.div(there, ngy), lax.rem(there, ngy)),
                            device_id_type=MESH)
        return 0

    lax.fori_loop(1, n, greet, 0)

    def bit_of(level):
        if level < bits_gy:
            return lax.rem(lax.div(gy, 2**level), 2)
        return lax.rem(lax.div(gx, 2 ** (level - bits_gy)), 2)

    def exchange(level, c):
        bit = bit_of(level)
        if level < bits_gy:
            there = (gx, gy + 2**level * (1 - 2 * bit))
        else:
            there = (gx + 2 ** (level - bits_gy) * (1 - 2 * bit), gy)
        return pltpu.make_async_remote_copy(
            src_ref=held.at[level, c], dst_ref=got.at[level, c],
            send_sem=send_sem.at[level, c], recv_sem=recv_sem.at[level, c],
            device_id=there, device_id_type=MESH)

    def prepare(level, k):
        real, imag = weights[level, 0, k], weights[level, 1, k]
        p = jnp.concatenate([real, imag], axis=0).T
        m = jnp.concatenate([-imag, real], axis=0).T
        low = jnp.concatenate([p[:rank], m[:rank]], axis=0)
        high = jnp.concatenate([p[rank:], m[rank:]], axis=0)
        first = bit_of(level) == 0
        own = jnp.where(first, low, high)
        other = jnp.where(first, high, low)
        hi, lo = split(jnp.concatenate([own, other], axis=0))
        wp[level, k] = jnp.concatenate([hi, lo], axis=1)

    def prepare_interp(k):
        real, imag = interp[0, k], interp[1, k]
        top = jnp.concatenate([real, imag], axis=1)
        low = jnp.concatenate([-imag, real], axis=1)
        hi, lo = split(jnp.concatenate([top, low], axis=0))
        ip[k] = jnp.concatenate([hi, lo], axis=1)

    def put(h, i):
        there = lax.rem(me + i, n)
        return pltpu.make_async_remote_copy(
            src_ref=stage.at[h, :, pl.ds(there * per, per)],
            dst_ref=out.at[:, pl.ds(h * per, per), pl.ds(me * boxes, boxes)],
            send_sem=put_sem.at[h, i], recv_sem=take_sem.at[h, me],
            device_id=(lax.div(there, ngy), lax.rem(there, ngy)), device_id_type=MESH)

    def take(h, i):
        there = lax.rem(me + i, n)
        return pltpu.make_async_remote_copy(
            src_ref=stage.at[h, :, pl.ds(there * per, per)],
            dst_ref=out.at[:, pl.ds(h * per, per), pl.ds(there * boxes, boxes)],
            send_sem=put_sem.at[h, i], recv_sem=take_sem.at[h, there],
            device_id=(lax.div(there, ngy), lax.rem(there, ngy)), device_id_type=MESH)

    def keep(h):
        return pltpu.make_async_copy(
            stage.at[h, :, pl.ds(me * per, per)],
            out.at[:, pl.ds(h * per, per), pl.ds(me * boxes, boxes)], own_sem.at[h])

    def turn(k, _):
        state = jnp.concatenate([source[0, k], source[1, k]], axis=0).T
        if halves == 1:
            held[0, k] = state
        else:
            state = state.reshape(n, halves, per, 2 * rank)
            for h in range(halves):
                held[0, h * boxes + k] = state[:, h].reshape(rows, 2 * rank)
        return 0

    lax.fori_loop(0, boxes, turn, 0)
    pl.semaphore_wait(barrier, n - 1)

    def first(c, _):
        exchange(0, c).start()
        return 0

    lax.fori_loop(0, chunks, first, 0)

    def work(level, c):
        h, k = lax.div(c, boxes), lax.rem(c, boxes)

        @pl.when(h == 0)
        def _():
            prepare(level, k)
            if level == levels - 1:
                prepare_interp(k)

        exchange(level, c).wait_recv()
        both = jnp.concatenate([held[level, c], got[level, c]], axis=1)
        state = mul3(both, wp[level, k], 2 * rank)
        if level < levels - 1:
            held[level + 1, c] = state
            exchange(level + 1, c).start()
            return
        samples = mul3(state, ip[k], 2 * q)
        for part in range(2):
            flat = stage.at[h, part].reshape(rows * boxes, q)
            flat[pl.ds(k, rows, stride=boxes), :] = samples[:, part * q:(part + 1) * q]

        @pl.when(k == boxes - 1)
        def _():
            def send(i, _):
                put(h, i).start()
                return 0

            lax.fori_loop(1, n, send, 0)
            keep(h).start()

    ahead, apart = 4, 2
    lag = [0] + [ahead + apart * (level - 1) for level in range(1, levels)]

    def tick(t, _):
        for level in range(levels):
            c = t - lag[level]

            @pl.when((t >= lag[level]) & (t < lag[level] + chunks))
            def _():
                work(level, c)

        return 0

    lax.fori_loop(0, chunks + lag[-1], tick, 0)

    def finish(c, _):
        for level in range(levels):
            exchange(level, c).wait_send()
        return 0

    lax.fori_loop(0, chunks, finish, 0)
    for h in range(halves):
        def end(i, _):
            put(h, i).wait_send()
            take(h, i).wait_recv()
            return 0

        lax.fori_loop(1, n, end, 0)
        keep(h).wait()


def solution(mesh):
    ngx, ngy = mesh.shape["gx"], mesh.shape["gy"]
    n = ngx * ngy

    def on_device(source, weights, interp):
        _, boxes, rank, frames = source.shape
        levels = weights.shape[0]
        q = interp.shape[3]
        each = frames // n
        halves = 2 if each % 16 == 0 else 1
        rows = frames // halves
        chunks = halves * boxes
        vmem = pl.BlockSpec(memory_space=pltpu.VMEM)
        return pl.pallas_call(
            functools.partial(kernel, ngx, ngy, halves),
            out_shape=jax.ShapeDtypeStruct((2, each, n * boxes, q), F32),
            in_specs=[vmem] * 3,
            out_specs=pl.BlockSpec(memory_space=pl.ANY),
            scratch_shapes=[
                pltpu.VMEM((levels, boxes, 4 * rank, 4 * rank), BF),
                pltpu.VMEM((boxes, 2 * rank, 4 * q), BF),
                pltpu.VMEM((levels, chunks, rows, 2 * rank), F32),
                pltpu.VMEM((levels, chunks, rows, 2 * rank), F32),
                pltpu.VMEM((halves, 2, rows, boxes, q), F32),
                pltpu.SemaphoreType.DMA((levels, chunks)),
                pltpu.SemaphoreType.DMA((levels, chunks)),
                pltpu.SemaphoreType.DMA((halves, n)),
                pltpu.SemaphoreType.DMA((halves, n)),
                pltpu.SemaphoreType.DMA((halves,)),
            ],
            compiler_params=pltpu.CompilerParams(
                collective_id=0, has_side_effects=True, vmem_limit_bytes=56 * 2**20),
        )(source, weights, interp)

    return jax.shard_map(
        on_device,
        mesh=mesh,
        in_specs=(
            P(None, ("gx", "gy"), None, None),
            P(None, None, ("gx", "gy"), None, None),
            P(None, ("gx", "gy"), None, None),
        ),
        out_specs=P(None, ("gx", "gy"), None, None),
        check_vma=False,
    )
```

```python
import functools

import jax
import jax.numpy as jnp
from jax import lax
from jax.experimental import pallas as pl
from jax.experimental.pallas import tpu as pltpu
from jax.sharding import PartitionSpec as P

MESH = pl.DeviceIdType.MESH
BF = jnp.bfloat16
F32 = jnp.float32
CORES = 2
SLOTS = 3


def split(x):
    hi = x.astype(BF)
    return hi, (x - hi.astype(F32)).astype(BF)


def mul3(x, both, width):
    hi, lo = split(x)
    wide = jnp.dot(hi, both, preferred_element_type=F32)
    return wide[:, :width] + (
        wide[:, width:] + jnp.dot(lo, both[:, :width], preferred_element_type=F32)
    )


def kernel(ngx, ngy, parts, source, weights, interp, out, wp, ip, held, got, zgot, igot,
           stage, turned, send_sem, recv_sem, zsend_sem, zrecv_sem, isend_sem, irecv_sem,
           put_sem, take_sem, own_sem):
    levels = weights.shape[0]
    boxes, rank, frames = source.shape[1:]
    q = interp.shape[3]
    nz = ngy // CORES
    plane = ngx * CORES
    each = frames // (ngx * ngy)
    per = each // parts
    rows = frames // parts
    zrows = rows // nz
    chunks = parts * boxes
    bits_gy = ngy.bit_length() - 1
    gx, gy = lax.axis_index("gx"), lax.axis_index("gy")
    z, core = lax.div(gy, CORES), lax.rem(gy, CORES)
    last = levels % SLOTS

    def at_z(where):
        return (gx, where * CORES + core)

    def in_plane(i):
        u = lax.rem(gx * CORES + core + i, plane)
        return lax.div(u, CORES), lax.rem(u, CORES)

    barrier = pltpu.get_barrier_semaphore()

    def greet_z(i, _):
        pl.semaphore_signal(barrier, inc=1, device_id=at_z(lax.rem(z + i, nz)),
                            device_id_type=MESH)
        return 0

    def greet_plane(i, _):
        x, c = in_plane(i)
        pl.semaphore_signal(barrier, inc=1, device_id=(x, z * CORES + c), device_id_type=MESH)
        return 0

    lax.fori_loop(1, nz, greet_z, 0)
    lax.fori_loop(1, plane, greet_plane, 0)

    def bit_of(level):
        if level < bits_gy:
            return lax.rem(lax.div(gy, 2**level), 2)
        return lax.rem(lax.div(gx, 2 ** (level - bits_gy)), 2)

    def exchange(level, c):
        bit = bit_of(level)
        if level < bits_gy:
            there = (gx, gy + 2**level * (1 - 2 * bit))
        else:
            there = (gx + 2 ** (level - bits_gy) * (1 - 2 * bit), gy)
        return pltpu.make_async_remote_copy(
            src_ref=held.at[level % SLOTS, c], dst_ref=got.at[level, c],
            send_sem=send_sem.at[level, c], recv_sem=recv_sem.at[level, c],
            device_id=there, device_id_type=MESH)

    def prepare(level, k):
        real, imag = weights[level, 0, k], weights[level, 1, k]
        p = jnp.concatenate([real, imag], axis=0).T
        m = jnp.concatenate([-imag, real], axis=0).T
        low = jnp.concatenate([p[:rank], m[:rank]], axis=0)
        high = jnp.concatenate([p[rank:], m[rank:]], axis=0)
        first = bit_of(level) == 0
        own = jnp.where(first, low, high)
        other = jnp.where(first, high, low)
        hi, lo = split(jnp.concatenate([own, other], axis=0))
        wp[level, k] = jnp.concatenate([hi, lo], axis=1)

    def prepare_interp(where, k):
        real, imag = igot[where, 0, k], igot[where, 1, k]
        top = jnp.concatenate([real, imag], axis=1)
        low = jnp.concatenate([-imag, real], axis=1)
        hi, lo = split(jnp.concatenate([top, low], axis=0))
        ip[where, k] = jnp.concatenate([hi, lo], axis=1)

    def pass_on(way, j):
        block = z - j if way == 0 else z + j
        there = z + 1 if way == 0 else z - 1
        return pltpu.make_async_remote_copy(
            src_ref=igot.at[block], dst_ref=igot.at[block],
            send_sem=isend_sem.at[way, j], recv_sem=irecv_sem.at[way, j + 1],
            device_id=at_z(there), device_id_type=MESH)

    def taken(way, j):
        block = z - j if way == 0 else z + j
        there = z - 1 if way == 0 else z + 1
        return pltpu.make_async_remote_copy(
            src_ref=igot.at[block], dst_ref=igot.at[block],
            send_sem=isend_sem.at[way, j - 1], recv_sem=irecv_sem.at[way, j],
            device_id=at_z(there), device_id_type=MESH)

    def sends(way, j):
        return ((z >= j) & (z + 1 < nz)) if way == 0 else ((z + j < nz) & (z >= 1))

    def takes(way, j):
        return (z >= j) if way == 0 else (z + j < nz)

    def gather_step(j):
        for way in range(2):
            if j > 0:
                @pl.when(takes(way, j))
                def _():
                    taken(way, j).wait_recv()
            if j < nz - 1:
                @pl.when(sends(way, j))
                def _():
                    pass_on(way, j).start()

    def over_z(c, j):
        there = lax.rem(z + j, nz)
        return pltpu.make_async_remote_copy(
            src_ref=held.at[last, c, pl.ds(pl.multiple_of(there * zrows, zrows), zrows)],
            dst_ref=zgot.at[c, z],
            send_sem=zsend_sem.at[c, j], recv_sem=zrecv_sem.at[c, z],
            device_id=at_z(there), device_id_type=MESH)

    def from_z(c, j):
        there = lax.rem(z + j, nz)
        return pltpu.make_async_remote_copy(
            src_ref=held.at[last, c, pl.ds(pl.multiple_of(there * zrows, zrows), zrows)],
            dst_ref=zgot.at[c, there],
            send_sem=zsend_sem.at[c, j], recv_sem=zrecv_sem.at[c, there],
            device_id=at_z(there), device_id_type=MESH)

    def put(h, i):
        x, c = in_plane(i)
        return pltpu.make_async_remote_copy(
            src_ref=stage.at[h, :, :, c, x],
            dst_ref=out.at[:, pl.ds(h * per, per), gx, :, core],
            send_sem=put_sem.at[h, i], recv_sem=take_sem.at[h, gx * CORES + core],
            device_id=(x, z * CORES + c), device_id_type=MESH)

    def take(h, i):
        x, c = in_plane(i)
        return pltpu.make_async_remote_copy(
            src_ref=stage.at[h, :, :, c, x],
            dst_ref=out.at[:, pl.ds(h * per, per), x, :, c],
            send_sem=put_sem.at[h, i], recv_sem=take_sem.at[h, x * CORES + c],
            device_id=(x, z * CORES + c), device_id_type=MESH)

    def keep(h):
        return pltpu.make_async_copy(
            stage.at[h, :, :, core, gx],
            out.at[:, pl.ds(h * per, per), gx, :, core], own_sem.at[h])

    def turn(k):
        turned[...] = jnp.concatenate([source[0, k], source[1, k]], axis=0).T
        for h in range(parts):
            for zz in range(nz):
                for i in range(per):
                    for c in range(CORES):
                        start = (zz * CORES + c) * each + h * per + i
                        to = zz * zrows + (i * CORES + c) * ngx
                        held[0, h * boxes + k, to:to + ngx, :] = turned[
                            pl.ds(start, ngx, stride=ngy * each), :]

    turn(0)
    igot[z] = interp[...]
    pl.semaphore_wait(barrier, nz - 1 + plane - 1)

    def begin(k, _):
        @pl.when(k > 0)
        def _():
            turn(k)

        for h in range(parts):
            exchange(0, h * boxes + k).start()
        return 0

    lax.fori_loop(0, boxes, begin, 0)

    def work(level, c):
        h, k = lax.div(c, boxes), lax.rem(c, boxes)

        @pl.when(h == 0)
        def _():
            prepare(level, k)

        exchange(level, c).wait_recv()
        both = jnp.concatenate([held[level % SLOTS, c], got[level, c]], axis=1)
        state = mul3(both, wp[level, k], 2 * rank)
        if level >= SLOTS - 1:
            exchange(level + 1 - SLOTS, c).wait_send()
        held[(level + 1) % SLOTS, c] = state
        if level < levels - 1:
            exchange(level + 1, c).start()
        else:
            for j in range(1, nz):
                over_z(c, j).start()
            zgot[c, z] = held[last, c, pl.ds(pl.multiple_of(z * zrows, zrows), zrows), :]

    def project(c):
        h, k = lax.div(c, boxes), lax.rem(c, boxes)

        @pl.when(h == 0)
        def _():
            for where in range(nz):
                prepare_interp(where, k)

        for j in range(1, nz):
            from_z(c, j).wait_recv()
        for where in range(nz):
            samples = mul3(zgot[c, where], ip[where, k], 2 * q)
            for part in range(2):
                flat = stage.at[h, part].reshape(rows * boxes, q)
                flat[pl.ds(where * boxes + k, zrows, stride=nz * boxes), :] = samples[
                    :, part * q:(part + 1) * q]

        @pl.when(k == boxes - 1)
        def _():
            def send(i, _):
                put(h, i).start()
                return 0

            lax.fori_loop(1, plane, send, 0)
            keep(h).start()

    ahead, apart = boxes, 3
    lag = [0] + [ahead + apart * (level - 1) for level in range(1, levels + 1)]

    def tick(t, _):
        for j in range(nz):
            @pl.when(t == j * lag[-1] // max(nz - 1, 1))
            def _():
                gather_step(j)

        for level in range(levels + 1):
            c = t - lag[level]

            @pl.when((t >= lag[level]) & (t < lag[level] + chunks))
            def _():
                if level < levels:
                    work(level, c)
                else:
                    project(c)

        return 0

    lax.fori_loop(0, chunks + lag[-1], tick, 0)

    def finish(c, _):
        for level in range(max(levels + 1 - SLOTS, 0), levels):
            exchange(level, c).wait_send()
        for j in range(1, nz):
            over_z(c, j).wait_send()
        return 0

    lax.fori_loop(0, chunks, finish, 0)
    for way in range(2):
        for j in range(nz - 1):
            @pl.when(sends(way, j))
            def _():
                pass_on(way, j).wait_send()

    def end(h, _):
        def one(i, _):
            put(h, i).wait_send()
            take(h, i).wait_recv()
            return 0

        lax.fori_loop(1, plane, one, 0)
        keep(h).wait()
        return 0

    lax.fori_loop(0, parts, end, 0)


def solution(mesh):
    ngx, ngy = mesh.shape["gx"], mesh.shape["gy"]
    n = ngx * ngy
    nz = ngy // CORES

    def on_device(source, weights, interp):
        _, boxes, rank, frames = source.shape
        levels = weights.shape[0]
        q = interp.shape[3]
        each = frames // n
        parts = 4 if each % 4 == 0 else 1
        rows = frames // parts
        chunks = parts * boxes
        vmem = pl.BlockSpec(memory_space=pltpu.VMEM)
        dma = pltpu.SemaphoreType.DMA
        result = pl.pallas_call(
            functools.partial(kernel, ngx, ngy, parts),
            out_shape=jax.ShapeDtypeStruct((2, each, ngx, nz, CORES, boxes, q), F32),
            in_specs=[vmem] * 3,
            out_specs=pl.BlockSpec(memory_space=pl.ANY),
            scratch_shapes=[
                pltpu.VMEM((levels, boxes, 4 * rank, 4 * rank), BF),
                pltpu.VMEM((nz, boxes, 2 * rank, 4 * q), BF),
                pltpu.VMEM((SLOTS, chunks, rows, 2 * rank), F32),
                pltpu.VMEM((levels, chunks, rows, 2 * rank), F32),
                pltpu.VMEM((chunks, nz, rows // nz, 2 * rank), F32),
                pltpu.VMEM((nz,) + interp.shape, F32),
                pltpu.VMEM((parts, 2, each // parts, CORES, ngx, nz, boxes, q), F32),
                pltpu.VMEM((frames, 2 * rank), F32),
                dma((levels, chunks)),
                dma((levels, chunks)),
                dma((chunks, nz)),
                dma((chunks, nz)),
                dma((2, nz)),
                dma((2, nz)),
                dma((parts, CORES * ngx)),
                dma((parts, CORES * ngx)),
                dma((parts,)),
            ],
            compiler_params=pltpu.CompilerParams(
                collective_id=0, has_side_effects=True, vmem_limit_bytes=60 * 2**20),
        )(source, weights, interp)
        return result.reshape(2, each, n * boxes, q)

    return jax.shard_map(
        on_device,
        mesh=mesh,
        in_specs=(
            P(None, ("gx", "gy"), None, None),
            P(None, None, ("gx", "gy"), None, None),
            P(None, ("gx", "gy"), None, None),
        ),
        out_specs=P(None, ("gx", "gy"), None, None),
        check_vma=False,
    )
```

```python
import functools

import jax
import jax.numpy as jnp
from jax import lax
from jax.experimental import pallas as pl
from jax.experimental.pallas import tpu as pltpu
from jax.sharding import PartitionSpec as P

MESH = pl.DeviceIdType.MESH
BF = jnp.bfloat16
F32 = jnp.float32
CORES = 2
SLOTS = 3
GROUP = 2


def split(x):
    hi = x.astype(BF)
    return hi, (x - hi.astype(F32)).astype(BF)


def mul3(x, both, width):
    hi, lo = split(x)
    wide = jnp.dot(hi, both, preferred_element_type=F32)
    return wide[:, :width] + (
        wide[:, width:] + jnp.dot(lo, both[:, :width], preferred_element_type=F32)
    )


def kernel(ngx, ngy, parts, source, weights, interp, out, wp, ip, held, got, zgot, igot,
           stage, turned, send_sem, recv_sem, zsend_sem, zrecv_sem, isend_sem, irecv_sem,
           put_sem, take_sem, own_sem):
    levels = weights.shape[0]
    boxes, rank, frames = source.shape[1:]
    q = interp.shape[3]
    nz = ngy // CORES
    plane = ngx * CORES
    each = frames // (ngx * ngy)
    per = each // parts
    rows = frames // parts
    zrows = rows // nz
    chunks = parts * boxes
    bits_gy = ngy.bit_length() - 1
    gx, gy = lax.axis_index("gx"), lax.axis_index("gy")
    z, core = lax.div(gy, CORES), lax.rem(gy, CORES)
    last = levels % SLOTS

    def at_z(where):
        return (gx, where * CORES + core)

    def in_plane(i):
        u = lax.rem(gx * CORES + core + i, plane)
        return lax.div(u, CORES), lax.rem(u, CORES)

    barrier = pltpu.get_barrier_semaphore()

    def greet_z(i, _):
        pl.semaphore_signal(barrier, inc=1, device_id=at_z(lax.rem(z + i, nz)),
                            device_id_type=MESH)
        return 0

    def greet_plane(i, _):
        x, c = in_plane(i)
        pl.semaphore_signal(barrier, inc=1, device_id=(x, z * CORES + c), device_id_type=MESH)
        return 0

    lax.fori_loop(1, nz, greet_z, 0)
    lax.fori_loop(1, plane, greet_plane, 0)

    def bit_of(level):
        if level < bits_gy:
            return lax.rem(lax.div(gy, 2**level), 2)
        return lax.rem(lax.div(gx, 2 ** (level - bits_gy)), 2)

    def exchange(level, c):
        bit = bit_of(level)
        if level < bits_gy:
            there = (gx, gy + 2**level * (1 - 2 * bit))
        else:
            there = (gx + 2 ** (level - bits_gy) * (1 - 2 * bit), gy)
        return pltpu.make_async_remote_copy(
            src_ref=held.at[level % SLOTS, c], dst_ref=got.at[level, c],
            send_sem=send_sem.at[level, c], recv_sem=recv_sem.at[level, c],
            device_id=there, device_id_type=MESH)

    def prepare(level, k):
        real, imag = weights[level, 0, k], weights[level, 1, k]
        p = jnp.concatenate([real, imag], axis=0).T
        m = jnp.concatenate([-imag, real], axis=0).T
        low = jnp.concatenate([p[:rank], m[:rank]], axis=0)
        high = jnp.concatenate([p[rank:], m[rank:]], axis=0)
        first = bit_of(level) == 0
        own = jnp.where(first, low, high)
        other = jnp.where(first, high, low)
        hi, lo = split(jnp.concatenate([own, other], axis=0))
        wp[level, k] = jnp.concatenate([hi, lo], axis=1)

    def prepare_interp(where, k):
        real, imag = igot[where, 0, k], igot[where, 1, k]
        top = jnp.concatenate([real, imag], axis=1)
        low = jnp.concatenate([-imag, real], axis=1)
        hi, lo = split(jnp.concatenate([top, low], axis=0))
        ip[where, k] = jnp.concatenate([hi, lo], axis=1)

    def pass_on(way, j):
        block = z - j if way == 0 else z + j
        there = z + 1 if way == 0 else z - 1
        return pltpu.make_async_remote_copy(
            src_ref=igot.at[block], dst_ref=igot.at[block],
            send_sem=isend_sem.at[way, j], recv_sem=irecv_sem.at[way, j + 1],
            device_id=at_z(there), device_id_type=MESH)

    def taken(way, j):
        block = z - j if way == 0 else z + j
        there = z - 1 if way == 0 else z + 1
        return pltpu.make_async_remote_copy(
            src_ref=igot.at[block], dst_ref=igot.at[block],
            send_sem=isend_sem.at[way, j - 1], recv_sem=irecv_sem.at[way, j],
            device_id=at_z(there), device_id_type=MESH)

    def sends(way, j):
        return ((z >= j) & (z + 1 < nz)) if way == 0 else ((z + j < nz) & (z >= 1))

    def takes(way, j):
        return (z >= j) if way == 0 else (z + j < nz)

    def gather_step(j):
        for way in range(2):
            if j > 0:
                @pl.when(takes(way, j))
                def _():
                    taken(way, j).wait_recv()
            if j < nz - 1:
                @pl.when(sends(way, j))
                def _():
                    pass_on(way, j).start()

    def over_z(c, j):
        there = lax.rem(z + j, nz)
        return pltpu.make_async_remote_copy(
            src_ref=held.at[last, c, pl.ds(pl.multiple_of(there * zrows, zrows), zrows)],
            dst_ref=zgot.at[c, z],
            send_sem=zsend_sem.at[c, j], recv_sem=zrecv_sem.at[c, z],
            device_id=at_z(there), device_id_type=MESH)

    def from_z(c, j):
        there = lax.rem(z + j, nz)
        return pltpu.make_async_remote_copy(
            src_ref=held.at[last, c, pl.ds(pl.multiple_of(there * zrows, zrows), zrows)],
            dst_ref=zgot.at[c, there],
            send_sem=zsend_sem.at[c, j], recv_sem=zrecv_sem.at[c, there],
            device_id=at_z(there), device_id_type=MESH)

    def put(h, i):
        x, c = in_plane(i)
        return pltpu.make_async_remote_copy(
            src_ref=stage.at[h, :, :, c, x],
            dst_ref=out.at[:, pl.ds(h * per, per), gx, :, core],
            send_sem=put_sem.at[h, i], recv_sem=take_sem.at[h, gx * CORES + core],
            device_id=(x, z * CORES + c), device_id_type=MESH)

    def take(h, i):
        x, c = in_plane(i)
        return pltpu.make_async_remote_copy(
            src_ref=stage.at[h, :, :, c, x],
            dst_ref=out.at[:, pl.ds(h * per, per), x, :, c],
            send_sem=put_sem.at[h, i], recv_sem=take_sem.at[h, x * CORES + c],
            device_id=(x, z * CORES + c), device_id_type=MESH)

    def keep(h):
        return pltpu.make_async_copy(
            stage.at[h, :, :, core, gx],
            out.at[:, pl.ds(h * per, per), gx, :, core], own_sem.at[h])

    def turn(k):
        turned[...] = jnp.concatenate([source[0, k], source[1, k]], axis=0).T
        for h in range(parts):
            for zz in range(nz):
                for i in range(per):
                    for c in range(CORES):
                        start = (zz * CORES + c) * each + h * per + i
                        to = zz * zrows + (i * CORES + c) * ngx
                        held[0, h * boxes + k, to:to + ngx, :] = turned[
                            pl.ds(start, ngx, stride=ngy * each), :]

    turn(0)
    igot[z] = interp[...]
    pl.semaphore_wait(barrier, nz - 1 + plane - 1)

    def begin(k, _):
        @pl.when(k > 0)
        def _():
            turn(k)

        for h in range(parts):
            exchange(0, h * boxes + k).start()
        return 0

    lax.fori_loop(0, boxes, begin, 0)

    def box(c):
        return lax.div(c, boxes), lax.rem(c, boxes)

    def work(level, step):
        group = [step * GROUP + g for g in range(GROUP)]

        @pl.when(step * GROUP < boxes)
        def _():
            for c in group:
                prepare(level, box(c)[1])

        for c in group:
            exchange(level, c).wait_recv()
            if level >= SLOTS - 1:
                exchange(level + 1 - SLOTS, c).wait_send()
        both = [jnp.concatenate([held[level % SLOTS, c], got[level, c]], axis=1) for c in group]
        blocks = [wp[level, box(c)[1]] for c in group]
        states = [mul3(x, w, 2 * rank) for x, w in zip(both, blocks)]
        for c, state in zip(group, states):
            held[(level + 1) % SLOTS, c] = state
        for c in group:
            if level < levels - 1:
                exchange(level + 1, c).start()
            else:
                for j in range(1, nz):
                    over_z(c, j).start()
                zgot[c, z] = held[last, c, pl.ds(pl.multiple_of(z * zrows, zrows), zrows), :]

    def project(step):
        group = [step * GROUP + g for g in range(GROUP)]

        @pl.when(step * GROUP < boxes)
        def _():
            for c in group:
                for where in range(nz):
                    prepare_interp(where, box(c)[1])

        for c in group:
            for j in range(1, nz):
                from_z(c, j).wait_recv()
        jobs = [(c, where) for c in group for where in range(nz)]
        samples = [mul3(zgot[c, where], ip[where, box(c)[1]], 2 * q) for c, where in jobs]
        for (c, where), sample in zip(jobs, samples):
            h, k = box(c)
            for part in range(2):
                flat = stage.at[h, part].reshape(rows * boxes, q)
                flat[pl.ds(where * boxes + k, zrows, stride=nz * boxes), :] = sample[
                    :, part * q:(part + 1) * q]

        h, k = box(group[-1])

        @pl.when(k == boxes - 1)
        def _():
            def send(i, _):
                put(h, i).start()
                return 0

            lax.fori_loop(1, plane, send, 0)
            keep(h).start()

    steps = chunks // GROUP
    lag = [0, 3, 5] + [7 + level for level in range(levels - 3)] + [levels + 5]

    def tick(t, _):
        for j in range(nz):
            @pl.when(t == j * lag[-1] // max(nz - 1, 1))
            def _():
                gather_step(j)

        for level in range(levels + 1):
            step = t - lag[level]

            @pl.when((t >= lag[level]) & (t < lag[level] + steps))
            def _():
                if level < levels:
                    work(level, step)
                else:
                    project(step)

        return 0

    lax.fori_loop(0, steps + lag[-1], tick, 0)

    def finish(c, _):
        for level in range(max(levels + 1 - SLOTS, 0), levels):
            exchange(level, c).wait_send()
        for j in range(1, nz):
            over_z(c, j).wait_send()
        return 0

    lax.fori_loop(0, chunks, finish, 0)
    for way in range(2):
        for j in range(nz - 1):
            @pl.when(sends(way, j))
            def _():
                pass_on(way, j).wait_send()

    def end(h, _):
        def one(i, _):
            put(h, i).wait_send()
            take(h, i).wait_recv()
            return 0

        lax.fori_loop(1, plane, one, 0)
        keep(h).wait()
        return 0

    lax.fori_loop(0, parts, end, 0)


def solution(mesh):
    ngx, ngy = mesh.shape["gx"], mesh.shape["gy"]
    n = ngx * ngy
    nz = ngy // CORES

    def on_device(source, weights, interp):
        _, boxes, rank, frames = source.shape
        levels = weights.shape[0]
        q = interp.shape[3]
        each = frames // n
        parts = 4 if each % 4 == 0 else 1
        rows = frames // parts
        chunks = parts * boxes
        vmem = pl.BlockSpec(memory_space=pltpu.VMEM)
        dma = pltpu.SemaphoreType.DMA
        result = pl.pallas_call(
            functools.partial(kernel, ngx, ngy, parts),
            out_shape=jax.ShapeDtypeStruct((2, each, ngx, nz, CORES, boxes, q), F32),
            in_specs=[vmem] * 3,
            out_specs=pl.BlockSpec(memory_space=pl.ANY),
            scratch_shapes=[
                pltpu.VMEM((levels, boxes, 4 * rank, 4 * rank), BF),
                pltpu.VMEM((nz, boxes, 2 * rank, 4 * q), BF),
                pltpu.VMEM((SLOTS, chunks, rows, 2 * rank), F32),
                pltpu.VMEM((levels, chunks, rows, 2 * rank), F32),
                pltpu.VMEM((chunks, nz, rows // nz, 2 * rank), F32),
                pltpu.VMEM((nz,) + interp.shape, F32),
                pltpu.VMEM((parts, 2, each // parts, CORES, ngx, nz, boxes, q), F32),
                pltpu.VMEM((frames, 2 * rank), F32),
                dma((levels, chunks)),
                dma((levels, chunks)),
                dma((chunks, nz)),
                dma((chunks, nz)),
                dma((2, nz)),
                dma((2, nz)),
                dma((parts, CORES * ngx)),
                dma((parts, CORES * ngx)),
                dma((parts,)),
            ],
            compiler_params=pltpu.CompilerParams(
                collective_id=0, has_side_effects=True, vmem_limit_bytes=60 * 2**20),
        )(source, weights, interp)
        return result.reshape(2, each, n * boxes, q)

    return jax.shard_map(
        on_device,
        mesh=mesh,
        in_specs=(
            P(None, ("gx", "gy"), None, None),
            P(None, None, ("gx", "gy"), None, None),
            P(None, ("gx", "gy"), None, None),
        ),
        out_specs=P(None, ("gx", "gy"), None, None),
        check_vma=False,
    )
```

```python
import functools

import jax
import jax.numpy as jnp
from jax import lax
from jax.experimental import pallas as pl
from jax.experimental.pallas import tpu as pltpu
from jax.sharding import PartitionSpec as P

MESH = pl.DeviceIdType.MESH
BF = jnp.bfloat16
F32 = jnp.float32
CORES = 2
SLOTS = 3
GROUP = 2


def split(x):
    hi = x.astype(BF)
    return hi, (x - hi.astype(F32)).astype(BF)


def mul3(x, both, width):
    hi, lo = split(x)
    wide = jnp.dot(hi, both, preferred_element_type=F32)
    return wide[:, :width] + (
        wide[:, width:] + jnp.dot(lo, both[:, :width], preferred_element_type=F32)
    )


def kernel(ngx, ngy, parts, source, weights, interp, out, wp, ip, held, got, zgot, igot,
           stage, turned, send_sem, recv_sem, zsend_sem, zrecv_sem, isend_sem, irecv_sem,
           put_sem, take_sem, own_sem):
    levels = weights.shape[0]
    boxes, rank, frames = source.shape[1:]
    q = interp.shape[3]
    nz = ngy // CORES
    plane = ngx * CORES
    each = frames // (ngx * ngy)
    per = each // parts
    rows = frames // parts
    zrows = rows // nz
    chunks = parts * boxes
    bits_gy = ngy.bit_length() - 1
    gx, gy = lax.axis_index("gx"), lax.axis_index("gy")
    z, core = lax.div(gy, CORES), lax.rem(gy, CORES)
    last = levels % SLOTS

    def at_z(where):
        return (gx, where * CORES + core)

    def in_plane(i):
        u = lax.rem(gx * CORES + core + i, plane)
        return lax.div(u, CORES), lax.rem(u, CORES)

    barrier = pltpu.get_barrier_semaphore()

    def greet_z(i, _):
        pl.semaphore_signal(barrier, inc=1, device_id=at_z(lax.rem(z + i, nz)),
                            device_id_type=MESH)
        return 0

    def greet_plane(i, _):
        x, c = in_plane(i)
        pl.semaphore_signal(barrier, inc=1, device_id=(x, z * CORES + c), device_id_type=MESH)
        return 0

    lax.fori_loop(1, nz, greet_z, 0)
    lax.fori_loop(1, plane, greet_plane, 0)

    def bit_of(level):
        if level < bits_gy:
            return lax.rem(lax.div(gy, 2**level), 2)
        return lax.rem(lax.div(gx, 2 ** (level - bits_gy)), 2)

    def exchange(level, c):
        bit = bit_of(level)
        if level < bits_gy:
            there = (gx, gy + 2**level * (1 - 2 * bit))
        else:
            there = (gx + 2 ** (level - bits_gy) * (1 - 2 * bit), gy)
        return pltpu.make_async_remote_copy(
            src_ref=held.at[level % SLOTS, c], dst_ref=got.at[level, c],
            send_sem=send_sem.at[level, c], recv_sem=recv_sem.at[level, c],
            device_id=there, device_id_type=MESH)

    def prepare(level, k):
        real, imag = weights[level, 0, k], weights[level, 1, k]
        p = jnp.concatenate([real, imag], axis=0).T
        m = jnp.concatenate([-imag, real], axis=0).T
        low = jnp.concatenate([p[:rank], m[:rank]], axis=0)
        high = jnp.concatenate([p[rank:], m[rank:]], axis=0)
        first = bit_of(level) == 0
        own = jnp.where(first, low, high)
        other = jnp.where(first, high, low)
        hi, lo = split(jnp.concatenate([own, other], axis=0))
        wp[level, k] = jnp.concatenate([hi, lo], axis=1)

    def prepare_interp(where, k):
        real, imag = igot[where, 0, k], igot[where, 1, k]
        top = jnp.concatenate([real, imag], axis=1)
        low = jnp.concatenate([-imag, real], axis=1)
        hi, lo = split(jnp.concatenate([top, low], axis=0))
        ip[where, k] = jnp.concatenate([hi, lo], axis=1)

    def pass_on(way, j):
        block = z - j if way == 0 else z + j
        there = z + 1 if way == 0 else z - 1
        return pltpu.make_async_remote_copy(
            src_ref=igot.at[block], dst_ref=igot.at[block],
            send_sem=isend_sem.at[way, j], recv_sem=irecv_sem.at[way, j + 1],
            device_id=at_z(there), device_id_type=MESH)

    def taken(way, j):
        block = z - j if way == 0 else z + j
        there = z - 1 if way == 0 else z + 1
        return pltpu.make_async_remote_copy(
            src_ref=igot.at[block], dst_ref=igot.at[block],
            send_sem=isend_sem.at[way, j - 1], recv_sem=irecv_sem.at[way, j],
            device_id=at_z(there), device_id_type=MESH)

    def sends(way, j):
        return ((z >= j) & (z + 1 < nz)) if way == 0 else ((z + j < nz) & (z >= 1))

    def takes(way, j):
        return (z >= j) if way == 0 else (z + j < nz)

    def gather_step(j):
        for way in range(2):
            if j > 0:
                @pl.when(takes(way, j))
                def _():
                    taken(way, j).wait_recv()
            if j < nz - 1:
                @pl.when(sends(way, j))
                def _():
                    pass_on(way, j).start()

    def over_z(c, j):
        there = lax.rem(z + j, nz)
        return pltpu.make_async_remote_copy(
            src_ref=held.at[last, c, pl.ds(pl.multiple_of(there * zrows, zrows), zrows)],
            dst_ref=zgot.at[c, z],
            send_sem=zsend_sem.at[c, j], recv_sem=zrecv_sem.at[c, z],
            device_id=at_z(there), device_id_type=MESH)

    def from_z(c, j):
        there = lax.rem(z + j, nz)
        return pltpu.make_async_remote_copy(
            src_ref=held.at[last, c, pl.ds(pl.multiple_of(there * zrows, zrows), zrows)],
            dst_ref=zgot.at[c, there],
            send_sem=zsend_sem.at[c, j], recv_sem=zrecv_sem.at[c, there],
            device_id=at_z(there), device_id_type=MESH)

    def put(h, i):
        x, c = in_plane(i)
        return pltpu.make_async_remote_copy(
            src_ref=stage.at[h, :, :, c, x],
            dst_ref=out.at[:, pl.ds(h * per, per), gx, :, core],
            send_sem=put_sem.at[h, i], recv_sem=take_sem.at[h, gx * CORES + core],
            device_id=(x, z * CORES + c), device_id_type=MESH)

    def take(h, i):
        x, c = in_plane(i)
        return pltpu.make_async_remote_copy(
            src_ref=stage.at[h, :, :, c, x],
            dst_ref=out.at[:, pl.ds(h * per, per), x, :, c],
            send_sem=put_sem.at[h, i], recv_sem=take_sem.at[h, x * CORES + c],
            device_id=(x, z * CORES + c), device_id_type=MESH)

    def keep(h):
        return pltpu.make_async_copy(
            stage.at[h, :, :, core, gx],
            out.at[:, pl.ds(h * per, per), gx, :, core], own_sem.at[h])

    def turn(k):
        turned[...] = jnp.concatenate([source[0, k], source[1, k]], axis=0).T
        for h in range(parts):
            for zz in range(nz):
                for i in range(per):
                    for c in range(CORES):
                        start = (zz * CORES + c) * each + h * per + i
                        to = zz * zrows + (i * CORES + c) * ngx
                        held[0, h * boxes + k, to:to + ngx, :] = turned[
                            pl.ds(start, ngx, stride=ngy * each), :]

    def begin(step):
        @pl.when(step > 0)
        def _():
            for g in range(GROUP):
                turn(step * GROUP + g)

        for h in range(parts):
            for g in range(GROUP):
                exchange(0, h * boxes + step * GROUP + g).start()

    def box(c):
        return lax.div(c, boxes), lax.rem(c, boxes)

    def work(level, step):
        group = [step * GROUP + g for g in range(GROUP)]

        @pl.when(step * GROUP < boxes)
        def _():
            for c in group:
                prepare(level, box(c)[1])

        for c in group:
            exchange(level, c).wait_recv()
            if level >= SLOTS - 1:
                exchange(level + 1 - SLOTS, c).wait_send()
        both = [jnp.concatenate([held[level % SLOTS, c], got[level, c]], axis=1) for c in group]
        blocks = [wp[level, box(c)[1]] for c in group]
        states = [mul3(x, w, 2 * rank) for x, w in zip(both, blocks)]
        for c, state in zip(group, states):
            held[(level + 1) % SLOTS, c] = state
        for c in group:
            if level < levels - 1:
                exchange(level + 1, c).start()
            else:
                for j in range(1, nz):
                    over_z(c, j).start()
                zgot[c, z] = held[last, c, pl.ds(pl.multiple_of(z * zrows, zrows), zrows), :]

    def project(step):
        group = [step * GROUP + g for g in range(GROUP)]

        @pl.when(step * GROUP < boxes)
        def _():
            for c in group:
                for where in range(nz):
                    prepare_interp(where, box(c)[1])

        for c in group:
            for j in range(1, nz):
                from_z(c, j).wait_recv()
        jobs = [(c, where) for c in group for where in range(nz)]
        samples = [mul3(zgot[c, where], ip[where, box(c)[1]], 2 * q) for c, where in jobs]
        for (c, where), sample in zip(jobs, samples):
            h, k = box(c)
            for part in range(2):
                flat = stage.at[h, part].reshape(rows * boxes, q)
                flat[pl.ds(where * boxes + k, zrows, stride=nz * boxes), :] = sample[
                    :, part * q:(part + 1) * q]

        h, k = box(group[-1])

        @pl.when(k == boxes - 1)
        def _():
            def send(i, _):
                put(h, i).start()
                return 0

            lax.fori_loop(1, plane, send, 0)
            keep(h).start()

    steps = chunks // GROUP
    lag = [1, 3, 5] + [7 + level for level in range(levels - 3)] + [levels + 5]
    gather_from, catch_up = 5, 16
    for g in range(GROUP):
        turn(g)
    igot[z] = interp[...]
    pl.semaphore_wait(barrier, nz - 1 + plane - 1)

    def projected(t):
        done = jnp.minimum(2 * (t - catch_up + 1), t - lag[-1] + 1)
        return jnp.clip(done, 0, steps)

    def tick(t, _):
        for j in range(nz):
            @pl.when(t == gather_from + j * (catch_up - gather_from) // max(nz - 1, 1))
            def _():
                gather_step(j)

        @pl.when(t < boxes // GROUP)
        def _():
            begin(t)

        for level in range(levels):
            step = t - lag[level]

            @pl.when((t >= lag[level]) & (t < lag[level] + steps))
            def _():
                work(level, step)

        def late(step, _):
            project(step)
            return 0

        lax.fori_loop(projected(t - 1), projected(t), late, 0)
        return 0

    lax.fori_loop(0, steps + lag[-1], tick, 0)

    def finish(c, _):
        for level in range(max(levels + 1 - SLOTS, 0), levels):
            exchange(level, c).wait_send()
        for j in range(1, nz):
            over_z(c, j).wait_send()
        return 0

    lax.fori_loop(0, chunks, finish, 0)
    for way in range(2):
        for j in range(nz - 1):
            @pl.when(sends(way, j))
            def _():
                pass_on(way, j).wait_send()

    def end(h, _):
        def one(i, _):
            put(h, i).wait_send()
            take(h, i).wait_recv()
            return 0

        lax.fori_loop(1, plane, one, 0)
        keep(h).wait()
        return 0

    lax.fori_loop(0, parts, end, 0)


def solution(mesh):
    ngx, ngy = mesh.shape["gx"], mesh.shape["gy"]
    n = ngx * ngy
    nz = ngy // CORES

    def on_device(source, weights, interp):
        _, boxes, rank, frames = source.shape
        levels = weights.shape[0]
        q = interp.shape[3]
        each = frames // n
        parts = 4 if each % 4 == 0 else 1
        rows = frames // parts
        chunks = parts * boxes
        vmem = pl.BlockSpec(memory_space=pltpu.VMEM)
        dma = pltpu.SemaphoreType.DMA
        result = pl.pallas_call(
            functools.partial(kernel, ngx, ngy, parts),
            out_shape=jax.ShapeDtypeStruct((2, each, ngx, nz, CORES, boxes, q), F32),
            in_specs=[vmem] * 3,
            out_specs=pl.BlockSpec(memory_space=pl.ANY),
            scratch_shapes=[
                pltpu.VMEM((levels, boxes, 4 * rank, 4 * rank), BF),
                pltpu.VMEM((nz, boxes, 2 * rank, 4 * q), BF),
                pltpu.VMEM((SLOTS, chunks, rows, 2 * rank), F32),
                pltpu.VMEM((levels, chunks, rows, 2 * rank), F32),
                pltpu.VMEM((chunks, nz, rows // nz, 2 * rank), F32),
                pltpu.VMEM((nz,) + interp.shape, F32),
                pltpu.VMEM((parts, 2, each // parts, CORES, ngx, nz, boxes, q), F32),
                pltpu.VMEM((frames, 2 * rank), F32),
                dma((levels, chunks)),
                dma((levels, chunks)),
                dma((chunks, nz)),
                dma((chunks, nz)),
                dma((2, nz)),
                dma((2, nz)),
                dma((parts, CORES * ngx)),
                dma((parts, CORES * ngx)),
                dma((parts,)),
            ],
            compiler_params=pltpu.CompilerParams(
                collective_id=0, has_side_effects=True, vmem_limit_bytes=60 * 2**20),
        )(source, weights, interp)
        return result.reshape(2, each, n * boxes, q)

    return jax.shard_map(
        on_device,
        mesh=mesh,
        in_specs=(
            P(None, ("gx", "gy"), None, None),
            P(None, None, ("gx", "gy"), None, None),
            P(None, ("gx", "gy"), None, None),
        ),
        out_specs=P(None, ("gx", "gy"), None, None),
        check_vma=False,
    )
```

```python
import functools

import jax
import jax.numpy as jnp
from jax import lax
from jax.experimental import pallas as pl
from jax.experimental.pallas import tpu as pltpu
from jax.sharding import PartitionSpec as P

MESH = pl.DeviceIdType.MESH
BF = jnp.bfloat16
F32 = jnp.float32
CORES = 2
SLOTS = 3
GROUP = 1


def split(x):
    hi = x.astype(BF)
    return hi, (x - hi.astype(F32)).astype(BF)


def mul3(x, both, width):
    hi, lo = split(x)
    wide = jnp.dot(hi, both, preferred_element_type=F32)
    return wide[:, :width] + (
        wide[:, width:] + jnp.dot(lo, both[:, :width], preferred_element_type=F32)
    )


def kernel(ngx, ngy, parts, source, weights, interp, out, wp, ip, held, got, zgot, igot,
           stage, turned, send_sem, recv_sem, zsend_sem, zrecv_sem, isend_sem, irecv_sem,
           put_sem, take_sem, own_sem):
    levels = weights.shape[0]
    boxes, rank, frames = source.shape[1:]
    q = interp.shape[3]
    nz = ngy // CORES
    plane = ngx * CORES
    each = frames // (ngx * ngy)
    per = each // parts
    rows = frames // parts
    zrows = rows // nz
    chunks = parts * boxes
    bits_gy = ngy.bit_length() - 1
    gx, gy = lax.axis_index("gx"), lax.axis_index("gy")
    z, core = lax.div(gy, CORES), lax.rem(gy, CORES)
    last = levels % SLOTS

    def at_z(where):
        return (gx, where * CORES + core)

    def in_plane(i):
        u = lax.rem(gx * CORES + core + i, plane)
        return lax.div(u, CORES), lax.rem(u, CORES)

    barrier = pltpu.get_barrier_semaphore()

    def greet_z(i, _):
        pl.semaphore_signal(barrier, inc=1, device_id=at_z(lax.rem(z + i, nz)),
                            device_id_type=MESH)
        return 0

    def greet_plane(i, _):
        x, c = in_plane(i)
        pl.semaphore_signal(barrier, inc=1, device_id=(x, z * CORES + c), device_id_type=MESH)
        return 0

    lax.fori_loop(1, nz, greet_z, 0)
    lax.fori_loop(1, plane, greet_plane, 0)

    def bit_of(level):
        if level < bits_gy:
            return lax.rem(lax.div(gy, 2**level), 2)
        return lax.rem(lax.div(gx, 2 ** (level - bits_gy)), 2)

    def exchange(level, c):
        bit = bit_of(level)
        if level < bits_gy:
            there = (gx, gy + 2**level * (1 - 2 * bit))
        else:
            there = (gx + 2 ** (level - bits_gy) * (1 - 2 * bit), gy)
        return pltpu.make_async_remote_copy(
            src_ref=held.at[level % SLOTS, c], dst_ref=got.at[level, c],
            send_sem=send_sem.at[level, c], recv_sem=recv_sem.at[level, c],
            device_id=there, device_id_type=MESH)

    def prepare(level, k):
        real, imag = weights[level, 0, k], weights[level, 1, k]
        p = jnp.concatenate([real, imag], axis=0).T
        m = jnp.concatenate([-imag, real], axis=0).T
        low = jnp.concatenate([p[:rank], m[:rank]], axis=0)
        high = jnp.concatenate([p[rank:], m[rank:]], axis=0)
        first = bit_of(level) == 0
        own = jnp.where(first, low, high)
        other = jnp.where(first, high, low)
        hi, lo = split(jnp.concatenate([own, other], axis=0))
        wp[level, k] = jnp.concatenate([hi, lo], axis=1)

    def prepare_interp(where, k):
        real, imag = igot[where, 0, k], igot[where, 1, k]
        top = jnp.concatenate([real, imag], axis=1)
        low = jnp.concatenate([-imag, real], axis=1)
        hi, lo = split(jnp.concatenate([top, low], axis=0))
        ip[where, k] = jnp.concatenate([hi, lo], axis=1)

    def pass_on(way, j):
        block = z - j if way == 0 else z + j
        there = z + 1 if way == 0 else z - 1
        return pltpu.make_async_remote_copy(
            src_ref=igot.at[block], dst_ref=igot.at[block],
            send_sem=isend_sem.at[way, j], recv_sem=irecv_sem.at[way, j + 1],
            device_id=at_z(there), device_id_type=MESH)

    def taken(way, j):
        block = z - j if way == 0 else z + j
        there = z - 1 if way == 0 else z + 1
        return pltpu.make_async_remote_copy(
            src_ref=igot.at[block], dst_ref=igot.at[block],
            send_sem=isend_sem.at[way, j - 1], recv_sem=irecv_sem.at[way, j],
            device_id=at_z(there), device_id_type=MESH)

    def sends(way, j):
        return ((z >= j) & (z + 1 < nz)) if way == 0 else ((z + j < nz) & (z >= 1))

    def takes(way, j):
        return (z >= j) if way == 0 else (z + j < nz)

    def gather_step(j):
        for way in range(2):
            if j > 0:
                @pl.when(takes(way, j))
                def _():
                    taken(way, j).wait_recv()
            if j < nz - 1:
                @pl.when(sends(way, j))
                def _():
                    pass_on(way, j).start()

    def over_z(c, j):
        there = lax.rem(z + j, nz)
        return pltpu.make_async_remote_copy(
            src_ref=held.at[last, c, pl.ds(pl.multiple_of(there * zrows, zrows), zrows)],
            dst_ref=zgot.at[c, z],
            send_sem=zsend_sem.at[c, j], recv_sem=zrecv_sem.at[c, z],
            device_id=at_z(there), device_id_type=MESH)

    def from_z(c, j):
        there = lax.rem(z + j, nz)
        return pltpu.make_async_remote_copy(
            src_ref=held.at[last, c, pl.ds(pl.multiple_of(there * zrows, zrows), zrows)],
            dst_ref=zgot.at[c, there],
            send_sem=zsend_sem.at[c, j], recv_sem=zrecv_sem.at[c, there],
            device_id=at_z(there), device_id_type=MESH)

    def put(h, i):
        x, c = in_plane(i)
        return pltpu.make_async_remote_copy(
            src_ref=stage.at[h, :, :, c, x],
            dst_ref=out.at[:, pl.ds(h * per, per), gx, :, core],
            send_sem=put_sem.at[h, i], recv_sem=take_sem.at[h, gx * CORES + core],
            device_id=(x, z * CORES + c), device_id_type=MESH)

    def take(h, i):
        x, c = in_plane(i)
        return pltpu.make_async_remote_copy(
            src_ref=stage.at[h, :, :, c, x],
            dst_ref=out.at[:, pl.ds(h * per, per), x, :, c],
            send_sem=put_sem.at[h, i], recv_sem=take_sem.at[h, x * CORES + c],
            device_id=(x, z * CORES + c), device_id_type=MESH)

    def keep(h):
        return pltpu.make_async_copy(
            stage.at[h, :, :, core, gx],
            out.at[:, pl.ds(h * per, per), gx, :, core], own_sem.at[h])

    def turn(k):
        turned[...] = jnp.concatenate([source[0, k], source[1, k]], axis=0).T
        for h in range(parts):
            for zz in range(nz):
                for i in range(per):
                    for c in range(CORES):
                        start = (zz * CORES + c) * each + h * per + i
                        to = zz * zrows + (i * CORES + c) * ngx
                        held[0, h * boxes + k, to:to + ngx, :] = turned[
                            pl.ds(start, ngx, stride=ngy * each), :]

    def begin(step):
        @pl.when(step > 0)
        def _():
            for g in range(GROUP):
                turn(step * GROUP + g)

        for h in range(parts):
            for g in range(GROUP):
                exchange(0, h * boxes + step * GROUP + g).start()

    def box(c):
        return lax.div(c, boxes), lax.rem(c, boxes)

    def work(level, step):
        group = [step * GROUP + g for g in range(GROUP)]

        @pl.when(step * GROUP < boxes)
        def _():
            for c in group:
                prepare(level, box(c)[1])

        for c in group:
            exchange(level, c).wait_recv()
            if level >= SLOTS - 1:
                exchange(level + 1 - SLOTS, c).wait_send()
        both = [jnp.concatenate([held[level % SLOTS, c], got[level, c]], axis=1) for c in group]
        blocks = [wp[level, box(c)[1]] for c in group]
        states = [mul3(x, w, 2 * rank) for x, w in zip(both, blocks)]
        for c, state in zip(group, states):
            held[(level + 1) % SLOTS, c] = state
        for c in group:
            if level < levels - 1:
                exchange(level + 1, c).start()
            else:
                for j in range(1, nz):
                    over_z(c, j).start()
                zgot[c, z] = held[last, c, pl.ds(pl.multiple_of(z * zrows, zrows), zrows), :]

    def project(step):
        group = [step * GROUP + g for g in range(GROUP)]

        @pl.when(step * GROUP < boxes)
        def _():
            for c in group:
                for where in range(nz):
                    prepare_interp(where, box(c)[1])

        for c in group:
            for j in range(1, nz):
                from_z(c, j).wait_recv()
        jobs = [(c, where) for c in group for where in range(nz)]
        samples = [mul3(zgot[c, where], ip[where, box(c)[1]], 2 * q) for c, where in jobs]
        for (c, where), sample in zip(jobs, samples):
            h, k = box(c)
            for part in range(2):
                flat = stage.at[h, part].reshape(rows * boxes, q)
                flat[pl.ds(where * boxes + k, zrows, stride=nz * boxes), :] = sample[
                    :, part * q:(part + 1) * q]

        h, k = box(group[-1])

        @pl.when(k == boxes - 1)
        def _():
            def send(i, _):
                put(h, i).start()
                return 0

            lax.fori_loop(1, plane, send, 0)
            keep(h).start()

    steps = chunks // GROUP
    lag = [1, 3, 5] + [7 + level for level in range(levels - 3)] + [levels + 5]
    gather_from, catch_up = 1, 13
    for g in range(GROUP):
        turn(g)
    igot[z] = interp[...]
    pl.semaphore_wait(barrier, nz - 1 + plane - 1)

    def projected(t):
        done = jnp.minimum(2 * (t - catch_up + 1), t - lag[-1] + 1)
        return jnp.clip(done, 0, steps)

    def tick(t, _):
        for j in range(nz):
            @pl.when(t == gather_from + j * (catch_up - gather_from) // max(nz - 1, 1))
            def _():
                gather_step(j)

        @pl.when(t < boxes // GROUP)
        def _():
            begin(t)

        for level in range(levels):
            step = t - lag[level]

            @pl.when((t >= lag[level]) & (t < lag[level] + steps))
            def _():
                work(level, step)

        def late(step, _):
            project(step)
            return 0

        lax.fori_loop(projected(t - 1), projected(t), late, 0)
        return 0

    lax.fori_loop(0, steps + lag[-1], tick, 0)

    def finish(c, _):
        for level in range(max(levels + 1 - SLOTS, 0), levels):
            exchange(level, c).wait_send()
        for j in range(1, nz):
            over_z(c, j).wait_send()
        return 0

    lax.fori_loop(0, chunks, finish, 0)
    for way in range(2):
        for j in range(nz - 1):
            @pl.when(sends(way, j))
            def _():
                pass_on(way, j).wait_send()

    def end(h, _):
        def one(i, _):
            put(h, i).wait_send()
            take(h, i).wait_recv()
            return 0

        lax.fori_loop(1, plane, one, 0)
        keep(h).wait()
        return 0

    lax.fori_loop(0, parts, end, 0)


def solution(mesh):
    ngx, ngy = mesh.shape["gx"], mesh.shape["gy"]
    n = ngx * ngy
    nz = ngy // CORES

    def on_device(source, weights, interp):
        _, boxes, rank, frames = source.shape
        levels = weights.shape[0]
        q = interp.shape[3]
        each = frames // n
        parts = 2 if each % 2 == 0 else 1
        rows = frames // parts
        chunks = parts * boxes
        vmem = pl.BlockSpec(memory_space=pltpu.VMEM)
        dma = pltpu.SemaphoreType.DMA
        result = pl.pallas_call(
            functools.partial(kernel, ngx, ngy, parts),
            out_shape=jax.ShapeDtypeStruct((2, each, ngx, nz, CORES, boxes, q), F32),
            in_specs=[vmem] * 3,
            out_specs=pl.BlockSpec(memory_space=pl.ANY),
            scratch_shapes=[
                pltpu.VMEM((levels, boxes, 4 * rank, 4 * rank), BF),
                pltpu.VMEM((nz, boxes, 2 * rank, 4 * q), BF),
                pltpu.VMEM((SLOTS, chunks, rows, 2 * rank), F32),
                pltpu.VMEM((levels, chunks, rows, 2 * rank), F32),
                pltpu.VMEM((chunks, nz, rows // nz, 2 * rank), F32),
                pltpu.VMEM((nz,) + interp.shape, F32),
                pltpu.VMEM((parts, 2, each // parts, CORES, ngx, nz, boxes, q), F32),
                pltpu.VMEM((frames, 2 * rank), F32),
                dma((levels, chunks)),
                dma((levels, chunks)),
                dma((chunks, nz)),
                dma((chunks, nz)),
                dma((2, nz)),
                dma((2, nz)),
                dma((parts, CORES * ngx)),
                dma((parts, CORES * ngx)),
                dma((parts,)),
            ],
            compiler_params=pltpu.CompilerParams(
                collective_id=0, has_side_effects=True, vmem_limit_bytes=60 * 2**20),
        )(source, weights, interp)
        return result.reshape(2, each, n * boxes, q)

    return jax.shard_map(
        on_device,
        mesh=mesh,
        in_specs=(
            P(None, ("gx", "gy"), None, None),
            P(None, None, ("gx", "gy"), None, None),
            P(None, ("gx", "gy"), None, None),
        ),
        out_specs=P(None, ("gx", "gy"), None, None),
        check_vma=False,
    )
```

```python
import functools

import jax
import jax.numpy as jnp
from jax import lax
from jax.experimental import pallas as pl
from jax.experimental.pallas import tpu as pltpu
from jax.sharding import PartitionSpec as P

MESH = pl.DeviceIdType.MESH
BF = jnp.bfloat16
F32 = jnp.float32
CORES = 2
SLOTS = 3
GROUP = 1


def split(x):
    hi = x.astype(BF)
    return hi, (x - hi.astype(F32)).astype(BF)


def mul3(x, both, width):
    hi, lo = split(x)
    wide = jnp.dot(hi, both, preferred_element_type=F32)
    return wide[:, :width] + (
        wide[:, width:] + jnp.dot(lo, both[:, :width], preferred_element_type=F32)
    )


def kernel(ngx, ngy, parts, source, weights, interp, out, wp, ip, held, got, zgot, igot,
           stage, turned, send_sem, recv_sem, zsend_sem, zrecv_sem, isend_sem, irecv_sem,
           put_sem, take_sem, own_sem):
    levels = weights.shape[0]
    boxes, rank, frames = source.shape[1:]
    q = interp.shape[3]
    nz = ngy // CORES
    plane = ngx * CORES
    each = frames // (ngx * ngy)
    per = each // parts
    rows = frames // parts
    zrows = rows // nz
    chunks = parts * boxes
    bits_gy = ngy.bit_length() - 1
    gx, gy = lax.axis_index("gx"), lax.axis_index("gy")
    z, core = lax.div(gy, CORES), lax.rem(gy, CORES)
    last = levels % SLOTS

    def at_z(where):
        return (gx, where * CORES + core)

    def in_plane(i):
        u = lax.rem(gx * CORES + core + i, plane)
        return lax.div(u, CORES), lax.rem(u, CORES)

    barrier = pltpu.get_barrier_semaphore()

    def greet_z(i, _):
        pl.semaphore_signal(barrier, inc=1, device_id=at_z(lax.rem(z + i, nz)),
                            device_id_type=MESH)
        return 0

    def greet_plane(i, _):
        x, c = in_plane(i)
        pl.semaphore_signal(barrier, inc=1, device_id=(x, z * CORES + c), device_id_type=MESH)
        return 0

    lax.fori_loop(1, nz, greet_z, 0)
    lax.fori_loop(1, plane, greet_plane, 0)

    def bit_of(level):
        if level < bits_gy:
            return lax.rem(lax.div(gy, 2**level), 2)
        return lax.rem(lax.div(gx, 2 ** (level - bits_gy)), 2)

    def exchange(level, c):
        bit = bit_of(level)
        if level < bits_gy:
            there = (gx, gy + 2**level * (1 - 2 * bit))
        else:
            there = (gx + 2 ** (level - bits_gy) * (1 - 2 * bit), gy)
        return pltpu.make_async_remote_copy(
            src_ref=held.at[level % SLOTS, c], dst_ref=got.at[level, c],
            send_sem=send_sem.at[level, c], recv_sem=recv_sem.at[level, c],
            device_id=there, device_id_type=MESH)

    def prepare(level, k):
        real, imag = weights[level, 0, k], weights[level, 1, k]
        p = jnp.concatenate([real, imag], axis=0).T
        m = jnp.concatenate([-imag, real], axis=0).T
        low = jnp.concatenate([p[:rank], m[:rank]], axis=0)
        high = jnp.concatenate([p[rank:], m[rank:]], axis=0)
        first = bit_of(level) == 0
        own = jnp.where(first, low, high)
        other = jnp.where(first, high, low)
        hi, lo = split(jnp.concatenate([own, other], axis=0))
        wp[level, k] = jnp.concatenate([hi, lo], axis=1)

    def prepare_interp(where, k):
        real, imag = igot[where, 0, k], igot[where, 1, k]
        top = jnp.concatenate([real, imag], axis=1)
        low = jnp.concatenate([-imag, real], axis=1)
        hi, lo = split(jnp.concatenate([top, low], axis=0))
        ip[where, k] = jnp.concatenate([hi, lo], axis=1)

    def pass_on(way, j):
        block = z - j if way == 0 else z + j
        there = z + 1 if way == 0 else z - 1
        return pltpu.make_async_remote_copy(
            src_ref=igot.at[block], dst_ref=igot.at[block],
            send_sem=isend_sem.at[way, j], recv_sem=irecv_sem.at[way, j + 1],
            device_id=at_z(there), device_id_type=MESH)

    def taken(way, j):
        block = z - j if way == 0 else z + j
        there = z - 1 if way == 0 else z + 1
        return pltpu.make_async_remote_copy(
            src_ref=igot.at[block], dst_ref=igot.at[block],
            send_sem=isend_sem.at[way, j - 1], recv_sem=irecv_sem.at[way, j],
            device_id=at_z(there), device_id_type=MESH)

    def sends(way, j):
        return ((z >= j) & (z + 1 < nz)) if way == 0 else ((z + j < nz) & (z >= 1))

    def takes(way, j):
        return (z >= j) if way == 0 else (z + j < nz)

    def gather_step(j):
        for way in range(2):
            if j > 0:
                @pl.when(takes(way, j))
                def _():
                    taken(way, j).wait_recv()
            if j < nz - 1:
                @pl.when(sends(way, j))
                def _():
                    pass_on(way, j).start()

    def over_z(c, j):
        there = lax.rem(z + j, nz)
        return pltpu.make_async_remote_copy(
            src_ref=held.at[last, c, pl.ds(pl.multiple_of(there * zrows, zrows), zrows)],
            dst_ref=zgot.at[c, z],
            send_sem=zsend_sem.at[c, j], recv_sem=zrecv_sem.at[c, z],
            device_id=at_z(there), device_id_type=MESH)

    def from_z(c, j):
        there = lax.rem(z + j, nz)
        return pltpu.make_async_remote_copy(
            src_ref=held.at[last, c, pl.ds(pl.multiple_of(there * zrows, zrows), zrows)],
            dst_ref=zgot.at[c, there],
            send_sem=zsend_sem.at[c, j], recv_sem=zrecv_sem.at[c, there],
            device_id=at_z(there), device_id_type=MESH)

    def put(h, i):
        x, c = in_plane(i)
        return pltpu.make_async_remote_copy(
            src_ref=stage.at[h, :, :, c, x],
            dst_ref=out.at[:, pl.ds(h * per, per), gx, :, core],
            send_sem=put_sem.at[h, i], recv_sem=take_sem.at[h, gx * CORES + core],
            device_id=(x, z * CORES + c), device_id_type=MESH)

    def take(h, i):
        x, c = in_plane(i)
        return pltpu.make_async_remote_copy(
            src_ref=stage.at[h, :, :, c, x],
            dst_ref=out.at[:, pl.ds(h * per, per), x, :, c],
            send_sem=put_sem.at[h, i], recv_sem=take_sem.at[h, x * CORES + c],
            device_id=(x, z * CORES + c), device_id_type=MESH)

    def keep(h):
        return pltpu.make_async_copy(
            stage.at[h, :, :, core, gx],
            out.at[:, pl.ds(h * per, per), gx, :, core], own_sem.at[h])

    def turn(k):
        turned[...] = jnp.concatenate([source[0, k], source[1, k]], axis=0).T
        for h in range(parts):
            for zz in range(nz):
                for i in range(per):
                    for c in range(CORES):
                        start = (zz * CORES + c) * each + h * per + i
                        to = zz * zrows + (i * CORES + c) * ngx
                        held[0, h * boxes + k, to:to + ngx, :] = turned[
                            pl.ds(start, ngx, stride=ngy * each), :]

    def begin(step):
        @pl.when(step > 0)
        def _():
            for g in range(GROUP):
                turn(step * GROUP + g)

        for h in range(parts):
            for g in range(GROUP):
                exchange(0, h * boxes + step * GROUP + g).start()

    def box(c):
        return lax.div(c, boxes), lax.rem(c, boxes)

    def work(level, step):
        group = [step * GROUP + g for g in range(GROUP)]

        @pl.when(step * GROUP < boxes)
        def _():
            for c in group:
                prepare(level, box(c)[1])

        for c in group:
            exchange(level, c).wait_recv()
            if level >= SLOTS - 1:
                exchange(level + 1 - SLOTS, c).wait_send()
        both = [jnp.concatenate([held[level % SLOTS, c], got[level, c]], axis=1) for c in group]
        blocks = [wp[level, box(c)[1]] for c in group]
        states = [mul3(x, w, 2 * rank) for x, w in zip(both, blocks)]
        for c, state in zip(group, states):
            held[(level + 1) % SLOTS, c] = state
        for c in group:
            if level < levels - 1:
                exchange(level + 1, c).start()
            else:
                for j in range(1, nz):
                    over_z(c, j).start()
                zgot[c, z] = held[last, c, pl.ds(pl.multiple_of(z * zrows, zrows), zrows), :]

    def project(step):
        group = [step * GROUP + g for g in range(GROUP)]

        @pl.when(step * GROUP < boxes)
        def _():
            for c in group:
                for where in range(nz):
                    prepare_interp(where, box(c)[1])

        for c in group:
            for j in range(1, nz):
                from_z(c, j).wait_recv()
        jobs = [(c, where) for c in group for where in range(nz)]
        samples = [mul3(zgot[c, where], ip[where, box(c)[1]], 2 * q) for c, where in jobs]
        for (c, where), sample in zip(jobs, samples):
            h, k = box(c)
            for part in range(2):
                flat = stage.at[h, part].reshape(rows * boxes, q)
                flat[pl.ds(where * boxes + k, zrows, stride=nz * boxes), :] = sample[
                    :, part * q:(part + 1) * q]

        h, k = box(group[-1])

        @pl.when(k == boxes - 1)
        def _():
            def send(i, _):
                put(h, i).start()
                return 0

            lax.fori_loop(1, plane, send, 0)
            keep(h).start()

    steps = chunks // GROUP
    lag = [1 + 2 * level for level in range(levels + 1)]
    shift = 3 * core + 2 * lax.rem(z, 2)
    gather_from, catch_up = 1, 13
    for g in range(GROUP):
        turn(g)
    igot[z] = interp[...]
    pl.semaphore_wait(barrier, nz - 1 + plane - 1)

    def projected(t):
        done = jnp.minimum(2 * (t - catch_up + 1), t - lag[-1] + 1)
        return jnp.clip(done, 0, steps)

    def tick(t, _):
        for j in range(nz):
            @pl.when(t == gather_from + j * (catch_up - gather_from) // max(nz - 1, 1))
            def _():
                gather_step(j)

        @pl.when(t < boxes // GROUP)
        def _():
            begin(t)

        def late(step, _):
            project(step)
            return 0

        def visit(i, _):
            turn_of = lax.rem(i + shift, levels + 1)
            for level in range(levels):
                step = t - lag[level]

                @pl.when((turn_of == level) & (t >= lag[level]) & (t < lag[level] + steps))
                def _():
                    work(level, step)

            @pl.when(turn_of == levels)
            def _():
                lax.fori_loop(projected(t - 1), projected(t), late, 0)

            return 0

        lax.fori_loop(0, levels + 1, visit, 0)
        return 0

    lax.fori_loop(0, steps + lag[-1], tick, 0)

    def finish(c, _):
        for level in range(max(levels + 1 - SLOTS, 0), levels):
            exchange(level, c).wait_send()
        for j in range(1, nz):
            over_z(c, j).wait_send()
        return 0

    lax.fori_loop(0, chunks, finish, 0)
    for way in range(2):
        for j in range(nz - 1):
            @pl.when(sends(way, j))
            def _():
                pass_on(way, j).wait_send()

    def end(h, _):
        def one(i, _):
            put(h, i).wait_send()
            take(h, i).wait_recv()
            return 0

        lax.fori_loop(1, plane, one, 0)
        keep(h).wait()
        return 0

    lax.fori_loop(0, parts, end, 0)


def solution(mesh):
    ngx, ngy = mesh.shape["gx"], mesh.shape["gy"]
    n = ngx * ngy
    nz = ngy // CORES

    def on_device(source, weights, interp):
        _, boxes, rank, frames = source.shape
        levels = weights.shape[0]
        q = interp.shape[3]
        each = frames // n
        parts = 2 if each % 2 == 0 else 1
        rows = frames // parts
        chunks = parts * boxes
        vmem = pl.BlockSpec(memory_space=pltpu.VMEM)
        dma = pltpu.SemaphoreType.DMA
        result = pl.pallas_call(
            functools.partial(kernel, ngx, ngy, parts),
            out_shape=jax.ShapeDtypeStruct((2, each, ngx, nz, CORES, boxes, q), F32),
            in_specs=[vmem] * 3,
            out_specs=pl.BlockSpec(memory_space=pl.ANY),
            scratch_shapes=[
                pltpu.VMEM((levels, boxes, 4 * rank, 4 * rank), BF),
                pltpu.VMEM((nz, boxes, 2 * rank, 4 * q), BF),
                pltpu.VMEM((SLOTS, chunks, rows, 2 * rank), F32),
                pltpu.VMEM((levels, chunks, rows, 2 * rank), F32),
                pltpu.VMEM((chunks, nz, rows // nz, 2 * rank), F32),
                pltpu.VMEM((nz,) + interp.shape, F32),
                pltpu.VMEM((parts, 2, each // parts, CORES, ngx, nz, boxes, q), F32),
                pltpu.VMEM((frames, 2 * rank), F32),
                dma((levels, chunks)),
                dma((levels, chunks)),
                dma((chunks, nz)),
                dma((chunks, nz)),
                dma((2, nz)),
                dma((2, nz)),
                dma((parts, CORES * ngx)),
                dma((parts, CORES * ngx)),
                dma((parts,)),
            ],
            compiler_params=pltpu.CompilerParams(
                collective_id=0, has_side_effects=True, vmem_limit_bytes=60 * 2**20),
        )(source, weights, interp)
        return result.reshape(2, each, n * boxes, q)

    return jax.shard_map(
        on_device,
        mesh=mesh,
        in_specs=(
            P(None, ("gx", "gy"), None, None),
            P(None, None, ("gx", "gy"), None, None),
            P(None, ("gx", "gy"), None, None),
        ),
        out_specs=P(None, ("gx", "gy"), None, None),
        check_vma=False,
    )
```

```python
import functools

import jax
import jax.numpy as jnp
from jax import lax
from jax.experimental import pallas as pl
from jax.experimental.pallas import tpu as pltpu
from jax.sharding import PartitionSpec as P

MESH = pl.DeviceIdType.MESH
BF = jnp.bfloat16
F32 = jnp.float32
CORES = 2
SLOTS = 3
GROUP = 2


def split(x):
    hi = x.astype(BF)
    return hi, (x - hi.astype(F32)).astype(BF)


def mul3(x, both, width):
    hi, lo = split(x)
    wide = jnp.dot(hi, both, preferred_element_type=F32)
    return wide[:, :width] + (
        wide[:, width:] + jnp.dot(lo, both[:, :width], preferred_element_type=F32)
    )


def kernel(ngx, ngy, parts, source, weights, interp, out, wp, ip, held, got, zgot, igot,
           stage, turned, send_sem, recv_sem, zsend_sem, zrecv_sem, isend_sem, irecv_sem,
           put_sem, take_sem, own_sem):
    levels = weights.shape[0]
    boxes, rank, frames = source.shape[1:]
    q = interp.shape[3]
    nz = ngy // CORES
    plane = ngx * CORES
    each = frames // (ngx * ngy)
    per = each // parts
    rows = frames // parts
    zrows = rows // nz
    chunks = parts * boxes
    bits_gy = ngy.bit_length() - 1
    gx, gy = lax.axis_index("gx"), lax.axis_index("gy")
    z, core = lax.div(gy, CORES), lax.rem(gy, CORES)
    last = levels % SLOTS

    def at_z(where):
        return (gx, where * CORES + core)

    def in_plane(i):
        u = lax.rem(gx * CORES + core + i, plane)
        return lax.div(u, CORES), lax.rem(u, CORES)

    barrier = pltpu.get_barrier_semaphore()

    def greet_z(i, _):
        pl.semaphore_signal(barrier, inc=1, device_id=at_z(lax.rem(z + i, nz)),
                            device_id_type=MESH)
        return 0

    def greet_plane(i, _):
        x, c = in_plane(i)
        pl.semaphore_signal(barrier, inc=1, device_id=(x, z * CORES + c), device_id_type=MESH)
        return 0

    lax.fori_loop(1, nz, greet_z, 0)
    lax.fori_loop(1, plane, greet_plane, 0)

    def bit_of(level):
        if level < bits_gy:
            return lax.rem(lax.div(gy, 2**level), 2)
        return lax.rem(lax.div(gx, 2 ** (level - bits_gy)), 2)

    def exchange(level, c):
        bit = bit_of(level)
        if level < bits_gy:
            there = (gx, gy + 2**level * (1 - 2 * bit))
        else:
            there = (gx + 2 ** (level - bits_gy) * (1 - 2 * bit), gy)
        return pltpu.make_async_remote_copy(
            src_ref=held.at[level % SLOTS, c], dst_ref=got.at[level, c],
            send_sem=send_sem.at[level, c], recv_sem=recv_sem.at[level, c],
            device_id=there, device_id_type=MESH)

    def prepare(level, k):
        real, imag = weights[level, 0, k], weights[level, 1, k]
        p = jnp.concatenate([real, imag], axis=0).T
        m = jnp.concatenate([-imag, real], axis=0).T
        low = jnp.concatenate([p[:rank], m[:rank]], axis=0)
        high = jnp.concatenate([p[rank:], m[rank:]], axis=0)
        first = bit_of(level) == 0
        own = jnp.where(first, low, high)
        other = jnp.where(first, high, low)
        hi, lo = split(jnp.concatenate([own, other], axis=0))
        wp[level, k] = jnp.concatenate([hi, lo], axis=1)

    def prepare_interp(where, k):
        real, imag = igot[where, k, 0], igot[where, k, 1]
        top = jnp.concatenate([real, imag], axis=1)
        low = jnp.concatenate([-imag, real], axis=1)
        hi, lo = split(jnp.concatenate([top, low], axis=0))
        ip[where, k] = jnp.concatenate([hi, lo], axis=1)

    def pass_on(way, j, k):
        block = z - j if way == 0 else z + j
        there = z + 1 if way == 0 else z - 1
        return pltpu.make_async_remote_copy(
            src_ref=igot.at[block, k], dst_ref=igot.at[block, k],
            send_sem=isend_sem.at[way, j, k], recv_sem=irecv_sem.at[way, j + 1, k],
            device_id=at_z(there), device_id_type=MESH)

    def taken(way, j, k):
        block = z - j if way == 0 else z + j
        there = z - 1 if way == 0 else z + 1
        return pltpu.make_async_remote_copy(
            src_ref=igot.at[block, k], dst_ref=igot.at[block, k],
            send_sem=isend_sem.at[way, j - 1, k], recv_sem=irecv_sem.at[way, j, k],
            device_id=at_z(there), device_id_type=MESH)

    def sends(way, j):
        return ((z >= j) & (z + 1 < nz)) if way == 0 else ((z + j < nz) & (z >= 1))

    def takes(way, j):
        return (z >= j) if way == 0 else (z + j < nz)

    def gather_step(j, step):
        for way in range(2):
            for g in range(GROUP):
                k = step * GROUP + g
                if j > 0:
                    @pl.when(takes(way, j))
                    def _():
                        taken(way, j, k).wait_recv()
                if j < nz - 1:
                    @pl.when(sends(way, j))
                    def _():
                        pass_on(way, j, k).start()

    def over_z(c, j):
        there = lax.rem(z + j, nz)
        return pltpu.make_async_remote_copy(
            src_ref=held.at[last, c, pl.ds(pl.multiple_of(there * zrows, zrows), zrows)],
            dst_ref=zgot.at[c, z],
            send_sem=zsend_sem.at[c, j], recv_sem=zrecv_sem.at[c, z],
            device_id=at_z(there), device_id_type=MESH)

    def from_z(c, j):
        there = lax.rem(z + j, nz)
        return pltpu.make_async_remote_copy(
            src_ref=held.at[last, c, pl.ds(pl.multiple_of(there * zrows, zrows), zrows)],
            dst_ref=zgot.at[c, there],
            send_sem=zsend_sem.at[c, j], recv_sem=zrecv_sem.at[c, there],
            device_id=at_z(there), device_id_type=MESH)

    def put(h, i):
        x, c = in_plane(i)
        return pltpu.make_async_remote_copy(
            src_ref=stage.at[h, :, :, c, x],
            dst_ref=out.at[:, pl.ds(h * per, per), gx, :, core],
            send_sem=put_sem.at[h, i], recv_sem=take_sem.at[h, gx * CORES + core],
            device_id=(x, z * CORES + c), device_id_type=MESH)

    def take(h, i):
        x, c = in_plane(i)
        return pltpu.make_async_remote_copy(
            src_ref=stage.at[h, :, :, c, x],
            dst_ref=out.at[:, pl.ds(h * per, per), x, :, c],
            send_sem=put_sem.at[h, i], recv_sem=take_sem.at[h, x * CORES + c],
            device_id=(x, z * CORES + c), device_id_type=MESH)

    def keep(h):
        return pltpu.make_async_copy(
            stage.at[h, :, :, core, gx],
            out.at[:, pl.ds(h * per, per), gx, :, core], own_sem.at[h])

    def turn(k):
        turned[...] = jnp.concatenate([source[0, k], source[1, k]], axis=0).T
        for h in range(parts):
            for zz in range(nz):
                for i in range(per):
                    for c in range(CORES):
                        start = (zz * CORES + c) * each + h * per + i
                        to = zz * zrows + (i * CORES + c) * ngx
                        held[0, h * boxes + k, to:to + ngx, :] = turned[
                            pl.ds(start, ngx, stride=ngy * each), :]

    def begin(step):
        @pl.when(step > 0)
        def _():
            for g in range(GROUP):
                turn(step * GROUP + g)

        for h in range(parts):
            for g in range(GROUP):
                exchange(0, h * boxes + step * GROUP + g).start()

    def box(c):
        return lax.div(c, boxes), lax.rem(c, boxes)

    def work(level, step):
        group = [step * GROUP + g for g in range(GROUP)]

        @pl.when(step * GROUP < boxes)
        def _():
            for c in group:
                prepare(level, box(c)[1])

        for c in group:
            exchange(level, c).wait_recv()
            if level >= SLOTS - 1:
                exchange(level + 1 - SLOTS, c).wait_send()
        both = [jnp.concatenate([held[level % SLOTS, c], got[level, c]], axis=1) for c in group]
        blocks = [wp[level, box(c)[1]] for c in group]
        states = [mul3(x, w, 2 * rank) for x, w in zip(both, blocks)]
        for c, state in zip(group, states):
            held[(level + 1) % SLOTS, c] = state
        for c in group:
            if level < levels - 1:
                exchange(level + 1, c).start()
            else:
                for j in range(1, nz):
                    over_z(c, j).start()
                zgot[c, z] = held[last, c, pl.ds(pl.multiple_of(z * zrows, zrows), zrows), :]

    def project(step):
        group = [step * GROUP + g for g in range(GROUP)]

        @pl.when(step * GROUP < boxes)
        def _():
            for c in group:
                for where in range(nz):
                    prepare_interp(where, box(c)[1])

        for c in group:
            for j in range(1, nz):
                from_z(c, j).wait_recv()
        jobs = [(c, where) for c in group for where in range(nz)]
        samples = [mul3(zgot[c, where], ip[where, box(c)[1]], 2 * q) for c, where in jobs]
        for (c, where), sample in zip(jobs, samples):
            h, k = box(c)
            for part in range(2):
                flat = stage.at[h, part].reshape(rows * boxes, q)
                flat[pl.ds(where * boxes + k, zrows, stride=nz * boxes), :] = sample[
                    :, part * q:(part + 1) * q]

        h, k = box(group[-1])

        @pl.when(k == boxes - 1)
        def _():
            def send(i, _):
                put(h, i).start()
                return 0

            lax.fori_loop(1, plane, send, 0)
            keep(h).start()

    steps = chunks // GROUP
    lag = [1, 3, 5] + [7 + level for level in range(levels - 3)] + [levels + 5]
    gap = (lag[-1] - 1) // max(nz - 1, 1)
    for g in range(GROUP):
        turn(g)
    for k in range(boxes):
        for part in range(2):
            igot[z, k, part] = interp[part, k]
    pl.semaphore_wait(barrier, nz - 1 + plane - 1)

    def tick(t, _):
        @pl.when(t < boxes // GROUP)
        def _():
            begin(t)

        for level in range(levels + 1):
            step = t - lag[level]

            @pl.when((t >= lag[level]) & (t < lag[level] + steps))
            def _():
                if level < levels:
                    work(level, step)
                else:
                    project(step)

            if level == min(2, levels):
                for j in range(nz):
                    start = 1 + j * gap

                    @pl.when((t >= start) & (t < start + boxes // GROUP))
                    def _():
                        gather_step(j, t - start)

        return 0

    lax.fori_loop(0, steps + lag[-1], tick, 0)

    def finish(c, _):
        for level in range(max(levels + 1 - SLOTS, 0), levels):
            exchange(level, c).wait_send()
        for j in range(1, nz):
            over_z(c, j).wait_send()
        return 0

    lax.fori_loop(0, chunks, finish, 0)
    for way in range(2):
        for j in range(nz - 1):
            @pl.when(sends(way, j))
            def _():
                for k in range(boxes):
                    pass_on(way, j, k).wait_send()

    def end(h, _):
        def one(i, _):
            put(h, i).wait_send()
            take(h, i).wait_recv()
            return 0

        lax.fori_loop(1, plane, one, 0)
        keep(h).wait()
        return 0

    lax.fori_loop(0, parts, end, 0)


def solution(mesh):
    ngx, ngy = mesh.shape["gx"], mesh.shape["gy"]
    n = ngx * ngy
    nz = ngy // CORES

    def on_device(source, weights, interp):
        _, boxes, rank, frames = source.shape
        levels = weights.shape[0]
        q = interp.shape[3]
        each = frames // n
        parts = 4 if each % 4 == 0 else 1
        rows = frames // parts
        chunks = parts * boxes
        vmem = pl.BlockSpec(memory_space=pltpu.VMEM)
        dma = pltpu.SemaphoreType.DMA
        result = pl.pallas_call(
            functools.partial(kernel, ngx, ngy, parts),
            out_shape=jax.ShapeDtypeStruct((2, each, ngx, nz, CORES, boxes, q), F32),
            in_specs=[vmem] * 3,
            out_specs=pl.BlockSpec(memory_space=pl.ANY),
            scratch_shapes=[
                pltpu.VMEM((levels, boxes, 4 * rank, 4 * rank), BF),
                pltpu.VMEM((nz, boxes, 2 * rank, 4 * q), BF),
                pltpu.VMEM((SLOTS, chunks, rows, 2 * rank), F32),
                pltpu.VMEM((levels, chunks, rows, 2 * rank), F32),
                pltpu.VMEM((chunks, nz, rows // nz, 2 * rank), F32),
                pltpu.VMEM((nz, boxes, 2, rank, q), F32),
                pltpu.VMEM((parts, 2, each // parts, CORES, ngx, nz, boxes, q), F32),
                pltpu.VMEM((frames, 2 * rank), F32),
                dma((levels, chunks)),
                dma((levels, chunks)),
                dma((chunks, nz)),
                dma((chunks, nz)),
                dma((2, nz, boxes)),
                dma((2, nz, boxes)),
                dma((parts, CORES * ngx)),
                dma((parts, CORES * ngx)),
                dma((parts,)),
            ],
            compiler_params=pltpu.CompilerParams(
                collective_id=0, has_side_effects=True, vmem_limit_bytes=60 * 2**20),
        )(source, weights, interp)
        return result.reshape(2, each, n * boxes, q)

    return jax.shard_map(
        on_device,
        mesh=mesh,
        in_specs=(
            P(None, ("gx", "gy"), None, None),
            P(None, None, ("gx", "gy"), None, None),
            P(None, ("gx", "gy"), None, None),
        ),
        out_specs=P(None, ("gx", "gy"), None, None),
        check_vma=False,
    )
```

```python
import functools

import jax
import jax.numpy as jnp
from jax import lax
from jax.experimental import pallas as pl
from jax.experimental.pallas import tpu as pltpu
from jax.sharding import PartitionSpec as P

MESH = pl.DeviceIdType.MESH
BF = jnp.bfloat16
F32 = jnp.float32
CORES = 2
SLOTS = 3
GROUP = 2


def split(x):
    hi = x.astype(BF)
    return hi, (x - hi.astype(F32)).astype(BF)


def mul3(x, both, width):
    hi, lo = split(x)
    wide = jnp.dot(hi, both, preferred_element_type=F32)
    return wide[:, :width] + (
        wide[:, width:] + jnp.dot(lo, both[:, :width], preferred_element_type=F32)
    )


def kernel(ngx, ngy, parts, source, weights, interp, out, wp, ip, held, got, zgot, igot,
           stage, turned, send_sem, recv_sem, zsend_sem, zrecv_sem, isend_sem, irecv_sem,
           put_sem, take_sem, own_sem):
    levels = weights.shape[0]
    boxes, rank, frames = source.shape[1:]
    q = interp.shape[3]
    nz = ngy // CORES
    plane = ngx * CORES
    each = frames // (ngx * ngy)
    per = each // parts
    rows = frames // parts
    zrows = rows // nz
    chunks = parts * boxes
    bits_gy = ngy.bit_length() - 1
    gx, gy = lax.axis_index("gx"), lax.axis_index("gy")
    z, core = lax.div(gy, CORES), lax.rem(gy, CORES)
    last = levels % SLOTS

    def at_z(where):
        return (gx, where * CORES + core)

    def in_plane(i):
        u = lax.rem(gx * CORES + core + i, plane)
        return lax.div(u, CORES), lax.rem(u, CORES)

    barrier = pltpu.get_barrier_semaphore()

    def greet_z(i, _):
        pl.semaphore_signal(barrier, inc=1, device_id=at_z(lax.rem(z + i, nz)),
                            device_id_type=MESH)
        return 0

    def greet_plane(i, _):
        x, c = in_plane(i)
        pl.semaphore_signal(barrier, inc=1, device_id=(x, z * CORES + c), device_id_type=MESH)
        return 0

    lax.fori_loop(1, nz, greet_z, 0)
    lax.fori_loop(1, plane, greet_plane, 0)

    def bit_of(level):
        if level < bits_gy:
            return lax.rem(lax.div(gy, 2**level), 2)
        return lax.rem(lax.div(gx, 2 ** (level - bits_gy)), 2)

    def exchange(level, c):
        bit = bit_of(level)
        if level < bits_gy:
            there = (gx, gy + 2**level * (1 - 2 * bit))
        else:
            there = (gx + 2 ** (level - bits_gy) * (1 - 2 * bit), gy)
        return pltpu.make_async_remote_copy(
            src_ref=held.at[level % SLOTS, c], dst_ref=got.at[level, c],
            send_sem=send_sem.at[level, c], recv_sem=recv_sem.at[level, c],
            device_id=there, device_id_type=MESH)

    def prepare(level, k):
        real, imag = weights[level, 0, k], weights[level, 1, k]
        p = jnp.concatenate([real, imag], axis=0).T
        m = jnp.concatenate([-imag, real], axis=0).T
        low = jnp.concatenate([p[:rank], m[:rank]], axis=0)
        high = jnp.concatenate([p[rank:], m[rank:]], axis=0)
        first = bit_of(level) == 0
        own = jnp.where(first, low, high)
        other = jnp.where(first, high, low)
        hi, lo = split(jnp.concatenate([own, other], axis=0))
        wp[level, k] = jnp.concatenate([hi, lo], axis=1)

    def prepare_interp(where, k):
        real, imag = igot[where, k, 0], igot[where, k, 1]
        top = jnp.concatenate([real, imag], axis=1)
        low = jnp.concatenate([-imag, real], axis=1)
        hi, lo = split(jnp.concatenate([top, low], axis=0))
        ip[where, k] = jnp.concatenate([hi, lo], axis=1)

    def pass_on(way, j, k):
        block = z - j if way == 0 else z + j
        there = z + 1 if way == 0 else z - 1
        return pltpu.make_async_remote_copy(
            src_ref=igot.at[block, k], dst_ref=igot.at[block, k],
            send_sem=isend_sem.at[way, j, k], recv_sem=irecv_sem.at[way, j + 1, k],
            device_id=at_z(there), device_id_type=MESH)

    def taken(way, j, k):
        block = z - j if way == 0 else z + j
        there = z - 1 if way == 0 else z + 1
        return pltpu.make_async_remote_copy(
            src_ref=igot.at[block, k], dst_ref=igot.at[block, k],
            send_sem=isend_sem.at[way, j - 1, k], recv_sem=irecv_sem.at[way, j, k],
            device_id=at_z(there), device_id_type=MESH)

    def sends(way, j):
        return ((z >= j) & (z + 1 < nz)) if way == 0 else ((z + j < nz) & (z >= 1))

    def takes(way, j):
        return (z >= j) if way == 0 else (z + j < nz)

    def gather_step(j, step):
        for way in range(2):
            for g in range(GROUP):
                k = step * GROUP + g
                if j > 0:
                    @pl.when(takes(way, j))
                    def _():
                        taken(way, j, k).wait_recv()
                if j < nz - 1:
                    @pl.when(sends(way, j))
                    def _():
                        pass_on(way, j, k).start()

    def over_z(c, j):
        there = lax.rem(z + j, nz)
        return pltpu.make_async_remote_copy(
            src_ref=held.at[last, c, pl.ds(pl.multiple_of(there * zrows, zrows), zrows)],
            dst_ref=zgot.at[c, z],
            send_sem=zsend_sem.at[c, j], recv_sem=zrecv_sem.at[c, z],
            device_id=at_z(there), device_id_type=MESH)

    def from_z(c, j):
        there = lax.rem(z + j, nz)
        return pltpu.make_async_remote_copy(
            src_ref=held.at[last, c, pl.ds(pl.multiple_of(there * zrows, zrows), zrows)],
            dst_ref=zgot.at[c, there],
            send_sem=zsend_sem.at[c, j], recv_sem=zrecv_sem.at[c, there],
            device_id=at_z(there), device_id_type=MESH)

    def put(h, i):
        x, c = in_plane(i)
        return pltpu.make_async_remote_copy(
            src_ref=stage.at[h, :, :, c, x],
            dst_ref=out.at[:, pl.ds(h * per, per), gx, :, core],
            send_sem=put_sem.at[h, i], recv_sem=take_sem.at[h, gx * CORES + core],
            device_id=(x, z * CORES + c), device_id_type=MESH)

    def take(h, i):
        x, c = in_plane(i)
        return pltpu.make_async_remote_copy(
            src_ref=stage.at[h, :, :, c, x],
            dst_ref=out.at[:, pl.ds(h * per, per), x, :, c],
            send_sem=put_sem.at[h, i], recv_sem=take_sem.at[h, x * CORES + c],
            device_id=(x, z * CORES + c), device_id_type=MESH)

    def keep(h):
        return pltpu.make_async_copy(
            stage.at[h, :, :, core, gx],
            out.at[:, pl.ds(h * per, per), gx, :, core], own_sem.at[h])

    def turn(k):
        turned[...] = jnp.concatenate([source[0, k], source[1, k]], axis=0).T
        for h in range(parts):
            for zz in range(nz):
                for i in range(per):
                    for c in range(CORES):
                        start = (zz * CORES + c) * each + h * per + i
                        to = zz * zrows + (i * CORES + c) * ngx
                        held[0, h * boxes + k, to:to + ngx, :] = turned[
                            pl.ds(start, ngx, stride=ngy * each), :]

    def begin(step):
        @pl.when(step > 0)
        def _():
            for g in range(GROUP):
                turn(step * GROUP + g)

        for h in range(parts):
            for g in range(GROUP):
                exchange(0, h * boxes + step * GROUP + g).start()

    def box(c):
        return lax.div(c, boxes), lax.rem(c, boxes)

    def work(level, step):
        group = [step * GROUP + g for g in range(GROUP)]

        @pl.when(step * GROUP < boxes)
        def _():
            for c in group:
                prepare(level, box(c)[1])

        for c in group:
            exchange(level, c).wait_recv()
            if level >= SLOTS - 1:
                exchange(level + 1 - SLOTS, c).wait_send()
        both = [jnp.concatenate([held[level % SLOTS, c], got[level, c]], axis=1) for c in group]
        blocks = [wp[level, box(c)[1]] for c in group]
        states = [mul3(x, w, 2 * rank) for x, w in zip(both, blocks)]
        for c, state in zip(group, states):
            held[(level + 1) % SLOTS, c] = state
        for c in group:
            if level < levels - 1:
                exchange(level + 1, c).start()
            else:
                for j in range(1, nz):
                    over_z(c, j).start()
                zgot[c, z] = held[last, c, pl.ds(pl.multiple_of(z * zrows, zrows), zrows), :]

    def project(step):
        group = [step * GROUP + g for g in range(GROUP)]

        @pl.when(step * GROUP < boxes)
        def _():
            for c in group:
                for where in range(nz):
                    prepare_interp(where, box(c)[1])

        for c in group:
            for j in range(1, nz):
                from_z(c, j).wait_recv()
        jobs = [(c, where) for c in group for where in range(nz)]
        samples = [mul3(zgot[c, where], ip[where, box(c)[1]], 2 * q) for c, where in jobs]
        for (c, where), sample in zip(jobs, samples):
            h, k = box(c)
            for part in range(2):
                flat = stage.at[h, part].reshape(rows * boxes, q)
                flat[pl.ds(where * boxes + k, zrows, stride=nz * boxes), :] = sample[
                    :, part * q:(part + 1) * q]

        h, k = box(group[-1])

        @pl.when(k == boxes - 1)
        def _():
            def send(i, _):
                put(h, i).start()
                return 0

            lax.fori_loop(1, plane, send, 0)
            keep(h).start()

    steps = chunks // GROUP
    lag = [1, 4, 8] + [11 + 2 * level for level in range(levels - 3)] + [2 * levels + 6]
    gap = (lag[-1] - 1) // max(nz - 1, 1)
    for g in range(GROUP):
        turn(g)
    for k in range(boxes):
        for part in range(2):
            igot[z, k, part] = interp[part, k]
    pl.semaphore_wait(barrier, nz - 1 + plane - 1)

    def tick(t, _):
        @pl.when(t < boxes // GROUP)
        def _():
            begin(t)

        for level in range(levels + 1):
            step = t - lag[level]

            @pl.when((t >= lag[level]) & (t < lag[level] + steps))
            def _():
                if level < levels:
                    work(level, step)
                else:
                    project(step)

            if level == min(2, levels):
                for j in range(nz):
                    start = 1 + j * gap

                    @pl.when((t >= start) & (t < start + boxes // GROUP))
                    def _():
                        gather_step(j, t - start)

        return 0

    lax.fori_loop(0, steps + lag[-1], tick, 0)

    def finish(c, _):
        for level in range(max(levels + 1 - SLOTS, 0), levels):
            exchange(level, c).wait_send()
        for j in range(1, nz):
            over_z(c, j).wait_send()
        return 0

    lax.fori_loop(0, chunks, finish, 0)
    for way in range(2):
        for j in range(nz - 1):
            @pl.when(sends(way, j))
            def _():
                for k in range(boxes):
                    pass_on(way, j, k).wait_send()

    def end(h, _):
        def one(i, _):
            put(h, i).wait_send()
            take(h, i).wait_recv()
            return 0

        lax.fori_loop(1, plane, one, 0)
        keep(h).wait()
        return 0

    lax.fori_loop(0, parts, end, 0)


def solution(mesh):
    ngx, ngy = mesh.shape["gx"], mesh.shape["gy"]
    n = ngx * ngy
    nz = ngy // CORES

    def on_device(source, weights, interp):
        _, boxes, rank, frames = source.shape
        levels = weights.shape[0]
        q = interp.shape[3]
        each = frames // n
        parts = 4 if each % 4 == 0 else 1
        rows = frames // parts
        chunks = parts * boxes
        vmem = pl.BlockSpec(memory_space=pltpu.VMEM)
        dma = pltpu.SemaphoreType.DMA
        result = pl.pallas_call(
            functools.partial(kernel, ngx, ngy, parts),
            out_shape=jax.ShapeDtypeStruct((2, each, ngx, nz, CORES, boxes, q), F32),
            in_specs=[vmem] * 3,
            out_specs=pl.BlockSpec(memory_space=pl.ANY),
            scratch_shapes=[
                pltpu.VMEM((levels, boxes, 4 * rank, 4 * rank), BF),
                pltpu.VMEM((nz, boxes, 2 * rank, 4 * q), BF),
                pltpu.VMEM((SLOTS, chunks, rows, 2 * rank), F32),
                pltpu.VMEM((levels, chunks, rows, 2 * rank), F32),
                pltpu.VMEM((chunks, nz, rows // nz, 2 * rank), F32),
                pltpu.VMEM((nz, boxes, 2, rank, q), F32),
                pltpu.VMEM((parts, 2, each // parts, CORES, ngx, nz, boxes, q), F32),
                pltpu.VMEM((frames, 2 * rank), F32),
                dma((levels, chunks)),
                dma((levels, chunks)),
                dma((chunks, nz)),
                dma((chunks, nz)),
                dma((2, nz, boxes)),
                dma((2, nz, boxes)),
                dma((parts, CORES * ngx)),
                dma((parts, CORES * ngx)),
                dma((parts,)),
            ],
            compiler_params=pltpu.CompilerParams(
                collective_id=0, has_side_effects=True, vmem_limit_bytes=60 * 2**20),
        )(source, weights, interp)
        return result.reshape(2, each, n * boxes, q)

    return jax.shard_map(
        on_device,
        mesh=mesh,
        in_specs=(
            P(None, ("gx", "gy"), None, None),
            P(None, None, ("gx", "gy"), None, None),
            P(None, ("gx", "gy"), None, None),
        ),
        out_specs=P(None, ("gx", "gy"), None, None),
        check_vma=False,
    )
```

```python
import functools

import jax
import jax.numpy as jnp
from jax import lax
from jax.experimental import pallas as pl
from jax.experimental.pallas import tpu as pltpu
from jax.sharding import PartitionSpec as P

MESH = pl.DeviceIdType.MESH
BF = jnp.bfloat16
F32 = jnp.float32
CORES = 2
SLOTS = 3
GROUP = 2


def split(x):
    hi = x.astype(BF)
    return hi, (x - hi.astype(F32)).astype(BF)


def mul3(x, both, width):
    hi, lo = split(x)
    wide = jnp.dot(hi, both, preferred_element_type=F32)
    return wide[:, :width] + (
        wide[:, width:] + jnp.dot(lo, both[:, :width], preferred_element_type=F32)
    )


def kernel(ngx, ngy, parts, source, weights, interp, out, wp, ip, held, got, zgot, igot,
           stage, turned, send_sem, recv_sem, zsend_sem, zrecv_sem, isend_sem, irecv_sem,
           put_sem, take_sem, own_sem):
    levels = weights.shape[0]
    boxes, rank, frames = source.shape[1:]
    q = interp.shape[3]
    nz = ngy // CORES
    plane = ngx * CORES
    each = frames // (ngx * ngy)
    per = each // parts
    rows = frames // parts
    zrows = rows // nz
    chunks = parts * boxes
    bits_gy = ngy.bit_length() - 1
    gx, gy = lax.axis_index("gx"), lax.axis_index("gy")
    z, core = lax.div(gy, CORES), lax.rem(gy, CORES)
    last = levels % SLOTS

    def at_z(where):
        return (gx, where * CORES + core)

    def in_plane(i):
        u = lax.rem(gx * CORES + core + i, plane)
        return lax.div(u, CORES), lax.rem(u, CORES)

    barrier = pltpu.get_barrier_semaphore()

    def greet_z(i, _):
        pl.semaphore_signal(barrier, inc=1, device_id=at_z(lax.rem(z + i, nz)),
                            device_id_type=MESH)
        return 0

    def greet_plane(i, _):
        x, c = in_plane(i)
        pl.semaphore_signal(barrier, inc=1, device_id=(x, z * CORES + c), device_id_type=MESH)
        return 0

    lax.fori_loop(1, nz, greet_z, 0)
    lax.fori_loop(1, plane, greet_plane, 0)

    def bit_of(level):
        if level < bits_gy:
            return lax.rem(lax.div(gy, 2**level), 2)
        return lax.rem(lax.div(gx, 2 ** (level - bits_gy)), 2)

    def exchange(level, c):
        bit = bit_of(level)
        if level < bits_gy:
            there = (gx, gy + 2**level * (1 - 2 * bit))
        else:
            there = (gx + 2 ** (level - bits_gy) * (1 - 2 * bit), gy)
        return pltpu.make_async_remote_copy(
            src_ref=held.at[level % SLOTS, c], dst_ref=got.at[level, c],
            send_sem=send_sem.at[level, c], recv_sem=recv_sem.at[level, c],
            device_id=there, device_id_type=MESH)

    def prepare(level, k):
        real, imag = weights[level, 0, k], weights[level, 1, k]
        p = jnp.concatenate([real, imag], axis=0).T
        m = jnp.concatenate([-imag, real], axis=0).T
        low = jnp.concatenate([p[:rank], m[:rank]], axis=0)
        high = jnp.concatenate([p[rank:], m[rank:]], axis=0)
        first = bit_of(level) == 0
        own = jnp.where(first, low, high)
        other = jnp.where(first, high, low)
        hi, lo = split(jnp.concatenate([own, other], axis=0))
        wp[level, k] = jnp.concatenate([hi, lo], axis=1)

    def prepare_interp(where, k):
        real, imag = igot[where, k, 0], igot[where, k, 1]
        top = jnp.concatenate([real, imag], axis=1)
        low = jnp.concatenate([-imag, real], axis=1)
        hi, lo = split(jnp.concatenate([top, low], axis=0))
        ip[where, k] = jnp.concatenate([hi, lo], axis=1)

    def pass_on(way, j, k):
        block = z - j if way == 0 else z + j
        there = z + 1 if way == 0 else z - 1
        return pltpu.make_async_remote_copy(
            src_ref=igot.at[block, k], dst_ref=igot.at[block, k],
            send_sem=isend_sem.at[way, j, k], recv_sem=irecv_sem.at[way, j + 1, k],
            device_id=at_z(there), device_id_type=MESH)

    def taken(way, j, k):
        block = z - j if way == 0 else z + j
        there = z - 1 if way == 0 else z + 1
        return pltpu.make_async_remote_copy(
            src_ref=igot.at[block, k], dst_ref=igot.at[block, k],
            send_sem=isend_sem.at[way, j - 1, k], recv_sem=irecv_sem.at[way, j, k],
            device_id=at_z(there), device_id_type=MESH)

    def sends(way, j):
        return ((z >= j) & (z + 1 < nz)) if way == 0 else ((z + j < nz) & (z >= 1))

    def takes(way, j):
        return (z >= j) if way == 0 else (z + j < nz)

    def gather_step(j, step):
        for way in range(2):
            for g in range(GROUP):
                k = step * GROUP + g
                if j > 0:
                    @pl.when(takes(way, j))
                    def _():
                        taken(way, j, k).wait_recv()
                if j < nz - 1:
                    @pl.when(sends(way, j))
                    def _():
                        pass_on(way, j, k).start()

    def over_z(c, j):
        there = lax.rem(z + j, nz)
        return pltpu.make_async_remote_copy(
            src_ref=held.at[last, c, pl.ds(pl.multiple_of(there * zrows, zrows), zrows)],
            dst_ref=zgot.at[c, z],
            send_sem=zsend_sem.at[c, j], recv_sem=zrecv_sem.at[c, z],
            device_id=at_z(there), device_id_type=MESH)

    def from_z(c, j):
        there = lax.rem(z + j, nz)
        return pltpu.make_async_remote_copy(
            src_ref=held.at[last, c, pl.ds(pl.multiple_of(there * zrows, zrows), zrows)],
            dst_ref=zgot.at[c, there],
            send_sem=zsend_sem.at[c, j], recv_sem=zrecv_sem.at[c, there],
            device_id=at_z(there), device_id_type=MESH)

    def put(h, i):
        x, c = in_plane(i)
        return pltpu.make_async_remote_copy(
            src_ref=stage.at[h, :, :, c, x],
            dst_ref=out.at[:, pl.ds(h * per, per), gx, :, core],
            send_sem=put_sem.at[h, i], recv_sem=take_sem.at[h, gx * CORES + core],
            device_id=(x, z * CORES + c), device_id_type=MESH)

    def take(h, i):
        x, c = in_plane(i)
        return pltpu.make_async_remote_copy(
            src_ref=stage.at[h, :, :, c, x],
            dst_ref=out.at[:, pl.ds(h * per, per), x, :, c],
            send_sem=put_sem.at[h, i], recv_sem=take_sem.at[h, x * CORES + c],
            device_id=(x, z * CORES + c), device_id_type=MESH)

    def keep(h):
        return pltpu.make_async_copy(
            stage.at[h, :, :, core, gx],
            out.at[:, pl.ds(h * per, per), gx, :, core], own_sem.at[h])

    def turn(k):
        turned[...] = jnp.concatenate([source[0, k], source[1, k]], axis=0).T
        for h in range(parts):
            for zz in range(nz):
                for i in range(per):
                    for c in range(CORES):
                        start = (zz * CORES + c) * each + h * per + i
                        to = zz * zrows + (i * CORES + c) * ngx
                        held[0, h * boxes + k, to:to + ngx, :] = turned[
                            pl.ds(start, ngx, stride=ngy * each), :]

    def begin(step):
        @pl.when(step > 0)
        def _():
            for g in range(GROUP):
                turn(step * GROUP + g)

        for h in range(parts):
            for g in range(GROUP):
                exchange(0, h * boxes + step * GROUP + g).start()

    def box(c):
        return lax.div(c, boxes), lax.rem(c, boxes)

    def work(level, step):
        group = [step * GROUP + g for g in range(GROUP)]

        @pl.when(step * GROUP < boxes)
        def _():
            for c in group:
                prepare(level, box(c)[1])

        for c in group:
            exchange(level, c).wait_recv()
            if level >= SLOTS - 1:
                exchange(level + 1 - SLOTS, c).wait_send()
        both = [jnp.concatenate([held[level % SLOTS, c], got[level, c]], axis=1) for c in group]
        blocks = [wp[level, box(c)[1]] for c in group]
        states = [mul3(x, w, 2 * rank) for x, w in zip(both, blocks)]
        for c, state in zip(group, states):
            held[(level + 1) % SLOTS, c] = state
        for c in group:
            if level < levels - 1:
                exchange(level + 1, c).start()
            else:
                for j in range(1, nz):
                    over_z(c, j).start()
                zgot[c, z] = held[last, c, pl.ds(pl.multiple_of(z * zrows, zrows), zrows), :]

    def project(step):
        group = [step * GROUP + g for g in range(GROUP)]

        @pl.when(step * GROUP < boxes)
        def _():
            for c in group:
                for where in range(nz):
                    prepare_interp(where, box(c)[1])

        for c in group:
            for j in range(1, nz):
                from_z(c, j).wait_recv()
        jobs = [(c, where) for c in group for where in range(nz)]
        samples = [mul3(zgot[c, where], ip[where, box(c)[1]], 2 * q) for c, where in jobs]
        for (c, where), sample in zip(jobs, samples):
            h, k = box(c)
            for part in range(2):
                flat = stage.at[h, part].reshape(rows * boxes, q)
                flat[pl.ds(where * boxes + k, zrows, stride=nz * boxes), :] = sample[
                    :, part * q:(part + 1) * q]

        h, k = box(group[-1])

        @pl.when(k == boxes - 1)
        def _():
            def send(i, _):
                put(h, i).start()
                return 0

            lax.fori_loop(1, plane, send, 0)
            keep(h).start()

    steps = chunks // GROUP
    lag = [1, 2] + [4 + level for level in range(levels - 1)]
    gap = (lag[-1] - 1) // max(nz - 1, 1)
    for g in range(GROUP):
        turn(g)
    for k in range(boxes):
        for part in range(2):
            igot[z, k, part] = interp[part, k]
    pl.semaphore_wait(barrier, nz - 1 + plane - 1)

    def tick(t, _):
        @pl.when(t < boxes // GROUP)
        def _():
            begin(t)

        for level in range(levels + 1):
            step = t - lag[level]

            @pl.when((t >= lag[level]) & (t < lag[level] + steps))
            def _():
                if level < levels:
                    work(level, step)
                else:
                    project(step)

            if level == min(2, levels):
                for j in range(nz):
                    start = 1 + j * gap

                    @pl.when((t >= start) & (t < start + boxes // GROUP))
                    def _():
                        gather_step(j, t - start)

        return 0

    lax.fori_loop(0, steps + lag[-1], tick, 0)

    def finish(c, _):
        for level in range(max(levels + 1 - SLOTS, 0), levels):
            exchange(level, c).wait_send()
        for j in range(1, nz):
            over_z(c, j).wait_send()
        return 0

    lax.fori_loop(0, chunks, finish, 0)
    for way in range(2):
        for j in range(nz - 1):
            @pl.when(sends(way, j))
            def _():
                for k in range(boxes):
                    pass_on(way, j, k).wait_send()

    def end(h, _):
        def one(i, _):
            put(h, i).wait_send()
            take(h, i).wait_recv()
            return 0

        lax.fori_loop(1, plane, one, 0)
        keep(h).wait()
        return 0

    lax.fori_loop(0, parts, end, 0)


def solution(mesh):
    ngx, ngy = mesh.shape["gx"], mesh.shape["gy"]
    n = ngx * ngy
    nz = ngy // CORES

    def on_device(source, weights, interp):
        _, boxes, rank, frames = source.shape
        levels = weights.shape[0]
        q = interp.shape[3]
        each = frames // n
        parts = 4 if each % 4 == 0 else 1
        rows = frames // parts
        chunks = parts * boxes
        vmem = pl.BlockSpec(memory_space=pltpu.VMEM)
        dma = pltpu.SemaphoreType.DMA
        result = pl.pallas_call(
            functools.partial(kernel, ngx, ngy, parts),
            out_shape=jax.ShapeDtypeStruct((2, each, ngx, nz, CORES, boxes, q), F32),
            in_specs=[vmem] * 3,
            out_specs=pl.BlockSpec(memory_space=pl.ANY),
            scratch_shapes=[
                pltpu.VMEM((levels, boxes, 4 * rank, 4 * rank), BF),
                pltpu.VMEM((nz, boxes, 2 * rank, 4 * q), BF),
                pltpu.VMEM((SLOTS, chunks, rows, 2 * rank), F32),
                pltpu.VMEM((levels, chunks, rows, 2 * rank), F32),
                pltpu.VMEM((chunks, nz, rows // nz, 2 * rank), F32),
                pltpu.VMEM((nz, boxes, 2, rank, q), F32),
                pltpu.VMEM((parts, 2, each // parts, CORES, ngx, nz, boxes, q), F32),
                pltpu.VMEM((frames, 2 * rank), F32),
                dma((levels, chunks)),
                dma((levels, chunks)),
                dma((chunks, nz)),
                dma((chunks, nz)),
                dma((2, nz, boxes)),
                dma((2, nz, boxes)),
                dma((parts, CORES * ngx)),
                dma((parts, CORES * ngx)),
                dma((parts,)),
            ],
            compiler_params=pltpu.CompilerParams(
                collective_id=0, has_side_effects=True, vmem_limit_bytes=60 * 2**20),
        )(source, weights, interp)
        return result.reshape(2, each, n * boxes, q)

    return jax.shard_map(
        on_device,
        mesh=mesh,
        in_specs=(
            P(None, ("gx", "gy"), None, None),
            P(None, None, ("gx", "gy"), None, None),
            P(None, ("gx", "gy"), None, None),
        ),
        out_specs=P(None, ("gx", "gy"), None, None),
        check_vma=False,
    )
```

```python
import functools

import jax
import jax.numpy as jnp
from jax import lax
from jax.experimental import pallas as pl
from jax.experimental.pallas import tpu as pltpu
from jax.sharding import PartitionSpec as P

MESH = pl.DeviceIdType.MESH
BF = jnp.bfloat16
F32 = jnp.float32
CORES = 2
SLOTS = 3
GROUP = 1


def split(x):
    hi = x.astype(BF)
    return hi, (x - hi.astype(F32)).astype(BF)


def mul3(x, both, width):
    hi, lo = split(x)
    wide = jnp.dot(hi, both, preferred_element_type=F32)
    return wide[:, :width] + (
        wide[:, width:] + jnp.dot(lo, both[:, :width], preferred_element_type=F32)
    )


def kernel(ngx, ngy, parts, source, weights, interp, out, wp, ip, held, got, zgot, igot,
           stage, turned, send_sem, recv_sem, zsend_sem, zrecv_sem, isend_sem, irecv_sem,
           put_sem, take_sem, own_sem):
    levels = weights.shape[0]
    boxes, rank, frames = source.shape[1:]
    q = interp.shape[3]
    nz = ngy // CORES
    plane = ngx * CORES
    each = frames // (ngx * ngy)
    per = each // parts
    rows = frames // parts
    zrows = rows // nz
    chunks = parts * boxes
    bits_gy = ngy.bit_length() - 1
    gx, gy = lax.axis_index("gx"), lax.axis_index("gy")
    z, core = lax.div(gy, CORES), lax.rem(gy, CORES)
    last = levels % SLOTS

    def at_z(where):
        return (gx, where * CORES + core)

    def in_plane(i):
        u = lax.rem(gx * CORES + core + i, plane)
        return lax.div(u, CORES), lax.rem(u, CORES)

    barrier = pltpu.get_barrier_semaphore()

    def greet_z(i, _):
        pl.semaphore_signal(barrier, inc=1, device_id=at_z(lax.rem(z + i, nz)),
                            device_id_type=MESH)
        return 0

    def greet_plane(i, _):
        x, c = in_plane(i)
        pl.semaphore_signal(barrier, inc=1, device_id=(x, z * CORES + c), device_id_type=MESH)
        return 0

    lax.fori_loop(1, nz, greet_z, 0)
    lax.fori_loop(1, plane, greet_plane, 0)

    def bit_of(level):
        if level < bits_gy:
            return lax.rem(lax.div(gy, 2**level), 2)
        return lax.rem(lax.div(gx, 2 ** (level - bits_gy)), 2)

    def exchange(level, c):
        bit = bit_of(level)
        if level < bits_gy:
            there = (gx, gy + 2**level * (1 - 2 * bit))
        else:
            there = (gx + 2 ** (level - bits_gy) * (1 - 2 * bit), gy)
        return pltpu.make_async_remote_copy(
            src_ref=held.at[level % SLOTS, c], dst_ref=got.at[level, c],
            send_sem=send_sem.at[level, c], recv_sem=recv_sem.at[level, c],
            device_id=there, device_id_type=MESH)

    def prepare(level, k):
        real, imag = weights[level, 0, k], weights[level, 1, k]
        p = jnp.concatenate([real, imag], axis=0).T
        m = jnp.concatenate([-imag, real], axis=0).T
        low = jnp.concatenate([p[:rank], m[:rank]], axis=0)
        high = jnp.concatenate([p[rank:], m[rank:]], axis=0)
        first = bit_of(level) == 0
        own = jnp.where(first, low, high)
        other = jnp.where(first, high, low)
        hi, lo = split(jnp.concatenate([own, other], axis=0))
        wp[level, k] = jnp.concatenate([hi, lo], axis=1)

    def prepare_interp(where, k):
        real, imag = igot[where, k, 0], igot[where, k, 1]
        top = jnp.concatenate([real, imag], axis=1)
        low = jnp.concatenate([-imag, real], axis=1)
        hi, lo = split(jnp.concatenate([top, low], axis=0))
        ip[where, k] = jnp.concatenate([hi, lo], axis=1)

    def pass_on(way, j, k):
        block = z - j if way == 0 else z + j
        there = z + 1 if way == 0 else z - 1
        return pltpu.make_async_remote_copy(
            src_ref=igot.at[block, k], dst_ref=igot.at[block, k],
            send_sem=isend_sem.at[way, j, k], recv_sem=irecv_sem.at[way, j + 1, k],
            device_id=at_z(there), device_id_type=MESH)

    def taken(way, j, k):
        block = z - j if way == 0 else z + j
        there = z - 1 if way == 0 else z + 1
        return pltpu.make_async_remote_copy(
            src_ref=igot.at[block, k], dst_ref=igot.at[block, k],
            send_sem=isend_sem.at[way, j - 1, k], recv_sem=irecv_sem.at[way, j, k],
            device_id=at_z(there), device_id_type=MESH)

    def sends(way, j):
        return ((z >= j) & (z + 1 < nz)) if way == 0 else ((z + j < nz) & (z >= 1))

    def takes(way, j):
        return (z >= j) if way == 0 else (z + j < nz)

    def gather_step(j, step):
        for way in range(2):
            for g in range(GROUP):
                k = step * GROUP + g
                if j > 0:
                    @pl.when(takes(way, j))
                    def _():
                        taken(way, j, k).wait_recv()
                if j < nz - 1:
                    @pl.when(sends(way, j))
                    def _():
                        pass_on(way, j, k).start()

    def over_z(c, j):
        there = lax.rem(z + j, nz)
        return pltpu.make_async_remote_copy(
            src_ref=held.at[last, c, pl.ds(pl.multiple_of(there * zrows, zrows), zrows)],
            dst_ref=zgot.at[c, z],
            send_sem=zsend_sem.at[c, j], recv_sem=zrecv_sem.at[c, z],
            device_id=at_z(there), device_id_type=MESH)

    def from_z(c, j):
        there = lax.rem(z + j, nz)
        return pltpu.make_async_remote_copy(
            src_ref=held.at[last, c, pl.ds(pl.multiple_of(there * zrows, zrows), zrows)],
            dst_ref=zgot.at[c, there],
            send_sem=zsend_sem.at[c, j], recv_sem=zrecv_sem.at[c, there],
            device_id=at_z(there), device_id_type=MESH)

    def put(h, i):
        x, c = in_plane(i)
        return pltpu.make_async_remote_copy(
            src_ref=stage.at[h, :, :, c, x],
            dst_ref=out.at[:, pl.ds(h * per, per), gx, :, core],
            send_sem=put_sem.at[h, i], recv_sem=take_sem.at[h, gx * CORES + core],
            device_id=(x, z * CORES + c), device_id_type=MESH)

    def take(h, i):
        x, c = in_plane(i)
        return pltpu.make_async_remote_copy(
            src_ref=stage.at[h, :, :, c, x],
            dst_ref=out.at[:, pl.ds(h * per, per), x, :, c],
            send_sem=put_sem.at[h, i], recv_sem=take_sem.at[h, x * CORES + c],
            device_id=(x, z * CORES + c), device_id_type=MESH)

    def keep(h):
        return pltpu.make_async_copy(
            stage.at[h, :, :, core, gx],
            out.at[:, pl.ds(h * per, per), gx, :, core], own_sem.at[h])

    def turn(k):
        turned[...] = jnp.concatenate([source[0, k], source[1, k]], axis=0).T
        for h in range(parts):
            for zz in range(nz):
                for i in range(per):
                    for c in range(CORES):
                        start = (zz * CORES + c) * each + h * per + i
                        to = zz * zrows + (i * CORES + c) * ngx
                        held[0, h * boxes + k, to:to + ngx, :] = turned[
                            pl.ds(start, ngx, stride=ngy * each), :]

    def begin(step):
        @pl.when(step > 0)
        def _():
            for g in range(GROUP):
                turn(step * GROUP + g)

        for h in range(parts):
            for g in range(GROUP):
                exchange(0, h * boxes + step * GROUP + g).start()

    def box(c):
        return lax.div(c, boxes), lax.rem(c, boxes)

    def work(level, step):
        group = [step * GROUP + g for g in range(GROUP)]

        @pl.when(step * GROUP < boxes)
        def _():
            for c in group:
                prepare(level, box(c)[1])

        for c in group:
            exchange(level, c).wait_recv()
            if level >= SLOTS - 1:
                exchange(level + 1 - SLOTS, c).wait_send()
        both = [jnp.concatenate([held[level % SLOTS, c], got[level, c]], axis=1) for c in group]
        blocks = [wp[level, box(c)[1]] for c in group]
        states = [mul3(x, w, 2 * rank) for x, w in zip(both, blocks)]
        for c, state in zip(group, states):
            held[(level + 1) % SLOTS, c] = state
        for c in group:
            if level < levels - 1:
                exchange(level + 1, c).start()
            else:
                for j in range(1, nz):
                    over_z(c, j).start()
                zgot[c, z] = held[last, c, pl.ds(pl.multiple_of(z * zrows, zrows), zrows), :]

    def project(step):
        group = [step * GROUP + g for g in range(GROUP)]

        @pl.when(step * GROUP < boxes)
        def _():
            for c in group:
                for where in range(nz):
                    prepare_interp(where, box(c)[1])

        for c in group:
            for j in range(1, nz):
                from_z(c, j).wait_recv()
        jobs = [(c, where) for c in group for where in range(nz)]
        samples = [mul3(zgot[c, where], ip[where, box(c)[1]], 2 * q) for c, where in jobs]
        for (c, where), sample in zip(jobs, samples):
            h, k = box(c)
            for part in range(2):
                flat = stage.at[h, part].reshape(rows * boxes, q)
                flat[pl.ds(where * boxes + k, zrows, stride=nz * boxes), :] = sample[
                    :, part * q:(part + 1) * q]

        h, k = box(group[-1])

        @pl.when(k == boxes - 1)
        def _():
            def send(i, _):
                put(h, i).start()
                return 0

            lax.fori_loop(1, plane, send, 0)
            keep(h).start()

    steps = chunks // GROUP
    lag = [1, 3, 5] + [7 + level for level in range(levels - 3)] + [levels + 5]
    gap = (lag[-1] - 1) // max(nz - 1, 1)
    for g in range(GROUP):
        turn(g)
    for k in range(boxes):
        for part in range(2):
            igot[z, k, part] = interp[part, k]
    pl.semaphore_wait(barrier, nz - 1 + plane - 1)

    def tick(t, _):
        @pl.when(t < boxes // GROUP)
        def _():
            begin(t)

        for level in range(levels + 1):
            step = t - lag[level]

            @pl.when((t >= lag[level]) & (t < lag[level] + steps))
            def _():
                if level < levels:
                    work(level, step)
                else:
                    project(step)

            if level == min(2, levels):
                for j in range(nz):
                    start = 1 + j * gap

                    @pl.when((t >= start) & (t < start + boxes // GROUP))
                    def _():
                        gather_step(j, t - start)

        return 0

    lax.fori_loop(0, steps + lag[-1], tick, 0)

    def finish(c, _):
        for level in range(max(levels + 1 - SLOTS, 0), levels):
            exchange(level, c).wait_send()
        for j in range(1, nz):
            over_z(c, j).wait_send()
        return 0

    lax.fori_loop(0, chunks, finish, 0)
    for way in range(2):
        for j in range(nz - 1):
            @pl.when(sends(way, j))
            def _():
                for k in range(boxes):
                    pass_on(way, j, k).wait_send()

    def end(h, _):
        def one(i, _):
            put(h, i).wait_send()
            take(h, i).wait_recv()
            return 0

        lax.fori_loop(1, plane, one, 0)
        keep(h).wait()
        return 0

    lax.fori_loop(0, parts, end, 0)


def solution(mesh):
    ngx, ngy = mesh.shape["gx"], mesh.shape["gy"]
    n = ngx * ngy
    nz = ngy // CORES

    def on_device(source, weights, interp):
        _, boxes, rank, frames = source.shape
        levels = weights.shape[0]
        q = interp.shape[3]
        each = frames // n
        parts = 2 if each % 2 == 0 else 1
        rows = frames // parts
        chunks = parts * boxes
        vmem = pl.BlockSpec(memory_space=pltpu.VMEM)
        dma = pltpu.SemaphoreType.DMA
        result = pl.pallas_call(
            functools.partial(kernel, ngx, ngy, parts),
            out_shape=jax.ShapeDtypeStruct((2, each, ngx, nz, CORES, boxes, q), F32),
            in_specs=[vmem] * 3,
            out_specs=pl.BlockSpec(memory_space=pl.ANY),
            scratch_shapes=[
                pltpu.VMEM((levels, boxes, 4 * rank, 4 * rank), BF),
                pltpu.VMEM((nz, boxes, 2 * rank, 4 * q), BF),
                pltpu.VMEM((SLOTS, chunks, rows, 2 * rank), F32),
                pltpu.VMEM((levels, chunks, rows, 2 * rank), F32),
                pltpu.VMEM((chunks, nz, rows // nz, 2 * rank), F32),
                pltpu.VMEM((nz, boxes, 2, rank, q), F32),
                pltpu.VMEM((parts, 2, each // parts, CORES, ngx, nz, boxes, q), F32),
                pltpu.VMEM((frames, 2 * rank), F32),
                dma((levels, chunks)),
                dma((levels, chunks)),
                dma((chunks, nz)),
                dma((chunks, nz)),
                dma((2, nz, boxes)),
                dma((2, nz, boxes)),
                dma((parts, CORES * ngx)),
                dma((parts, CORES * ngx)),
                dma((parts,)),
            ],
            compiler_params=pltpu.CompilerParams(
                collective_id=0, has_side_effects=True, vmem_limit_bytes=60 * 2**20),
        )(source, weights, interp)
        return result.reshape(2, each, n * boxes, q)

    return jax.shard_map(
        on_device,
        mesh=mesh,
        in_specs=(
            P(None, ("gx", "gy"), None, None),
            P(None, None, ("gx", "gy"), None, None),
            P(None, ("gx", "gy"), None, None),
        ),
        out_specs=P(None, ("gx", "gy"), None, None),
        check_vma=False,
    )
```
